32 devices in a mesh: req: 8 (over y, x, core), tp: 4 (over z).
Axes of the slice: x: 2, y: 2, z: 4, core: 2. Of those that a mesh axis runs over, the one named last changes fastest.
Arguments:
- hidden: bfloat16 [8, 128, 2048], P('req', None, 'tp'), may hold values from -600 to 600
- norm_gain: bfloat16 [2048], replicated, may hold values from 0.099609375 to 1.8984375
- w_query: bfloat16 [2048, 2048], P('req', 'tp'), may hold values from -0.125 to 0.125
- w_key: bfloat16 [2048, 512], P('req', 'tp'), may hold values from -0.125 to 0.125
- w_value: bfloat16 [2048, 512], P('req', 'tp'), may hold values from -0.125 to 0.125
- w_out: bfloat16 [2048, 2048], P('tp', 'req'), may hold values from -0.125 to 0.125
- cache_keys: bfloat16 [8, 2048, 512], P('req', None, 'tp'), may hold values from -72 to 72
- cache_values: bfloat16 [8, 2048, 512], P('req', None, 'tp'), may hold values from -6 to 6
- cache_lengths: int32 [8], replicated, may hold values from 1 to 2048, 8192 in all
Outputs:
- attn_out: bfloat16 [8, 128, 2048], P('req', None, 'tp')
- new_keys: bfloat16 [8, 128, 512], P('req', None, 'tp')
- new_values: bfloat16 [8, 128, 512], P('req', None, 'tp')
The draws below stay inside these ranges and needn't reach their ends.
Inputs may be any that keep to these rules, and one draw needn't show every extreme that they name: `cache_lengths`: one request has exactly 2048 cached positions; all requests together have 8 * 1024.
All inputs are finite; a program needn't handle non-finite values.
Results may differ from the reference program's by a relative error of at most 0.015.
Values may be sent and summed in bfloat16 or wider, within the bound.
No kernel may reach another device: no remote copies, remote signals or barrier semaphores. Data moves between devices by JAX's collectives and lax.ppermute only.
A program may use at most 64 MiB of HBM per device.

```python
import math
import jax
import jax.numpy as jnp
import numpy as np
from jax import lax

D = 2048
HEADS = 32
KVH = 8
HD = 64
TOK_DEV = 128
CACHE = 2048
REQS = 8
N_TP = 4


def draw_hidden(key, part):
    key_base, key_rows, key_cols = jax.random.split(key, 3)
    shape_full = (REQS, TOK_DEV, D)
    row_scale = jnp.exp(jax.random.uniform(key_rows, (REQS, TOK_DEV, 1), jnp.float32, 0.0, math.log(10.0)))
    col_scale = jnp.exp(jax.random.uniform(key_cols, (1, 1, D), jnp.float32, 0.0, math.log(10.0)))
    base_draw = jnp.clip(jax.random.normal(key_base, shape_full, jnp.float32), -6.0, 6.0)
    return (base_draw * row_scale * col_scale).astype(jnp.bfloat16)


def draw_cache_keys(key, part):
    key_base = jax.random.fold_in(key, 0)
    shape_full = (REQS, CACHE, KVH * HD)
    result_draw = jnp.clip(jax.random.normal(key_base, shape_full, jnp.float32), -4.0, 4.0)
    return result_draw.astype(jnp.bfloat16)


def block_scale(stream_key, shape, shards, low, top_value):
    level, own = 1.0, jax.random.fold_in(stream_key, 6)
    for position, parts in shards:
        draws = jnp.exp(jax.random.uniform(jax.random.fold_in(own, position), (parts,), jnp.float32, low / len(shards), top_value / len(shards)))
        level = level * jnp.repeat(draws, shape[position] // parts).reshape([-1 if axis == position else 1 for axis in range(len(shape))])
    return level


def profile(count, total, most, skew):
    portions = [(1 << 20) // math.isqrt(standing ** skew) + 1 for standing in range(2, count + 1)]
    spare, counts = total - most - (count - 1), [1] * (count - 1)
    while spare > 0:
        movable = [i for i in range(count - 1) if counts[i] < most]
        pool, budget = sum([portions[i] for i in movable]), spare
        for i in movable:
            extra = min(most - counts[i], max(1, budget * portions[i] // pool), spare)
            counts[i] = counts[i] + extra
            spare = spare - extra
    return np.array([most] + counts)


def uneven(key, amount, total, most, slope):
    if amount == 2:
        one = jax.random.randint(key, (), max(1, total - most), min(most, total - 1) + 1)
        return jnp.stack([one, total - one])
    sizes = jnp.asarray(profile(amount, total, most, slope), jnp.int32)
    twos = (amount - 1) // 2
    giver, taker = sizes[1:1 + 2 * twos:2], sizes[2:2 + 2 * twos:2]
    room = jnp.minimum(giver - 1, most - taker)
    passed = jax.random.randint(jax.random.fold_in(key, 1), (twos,), 0, 1 << 20) % (room + 1)
    sizes = sizes.at[1:1 + 2 * twos:2].set(giver - passed).at[2:2 + 2 * twos:2].set(taker + passed)
    return sizes[jax.random.permutation(jax.random.fold_in(key, 2), amount)]


def noise(key, extent, spread, bound, cuts=(), kind=jnp.bfloat16):
    factor_of = block_scale(key, extent, cuts, -0.22, 0.18) if cuts else 1.0
    values = jax.random.normal(key, extent, jnp.float32) * spread * factor_of
    return jnp.minimum(jnp.maximum(values, -bound), bound).astype(kind)


def setup_inputs(seed: int = 0) -> dict:
    key_of = jax.random.split(jax.random.key(seed), 10)
    hidden = draw_hidden(jax.random.fold_in(key_of[9], 71), 0)
    norm_gain = jnp.clip(1.0 + 0.18 * jax.random.normal(key_of[1], (D,), jnp.float32), 0.099609375, 1.8984375).astype(jnp.bfloat16)
    w_query = noise(key_of[2], (D, HEADS * HD), D ** -0.5, 0.125, ((0, 8), (1, 4)))
    w_key = noise(key_of[3], (D, KVH * HD), D ** -0.5, 0.125, ((0, 8), (1, 4)))
    w_value = noise(key_of[4], (D, KVH * HD), D ** -0.5, 0.125, ((0, 8), (1, 4)))
    w_out = noise(key_of[5], (HEADS * HD, D), (HEADS * HD) ** -0.5, 0.125, ((0, 4), (1, 8)))
    cache_keys = draw_cache_keys(jax.random.fold_in(key_of[9], 71), 0)
    cache_values = noise(key_of[7], (REQS, CACHE, KVH * HD), 1.0, 6.0, ((0, 8), (2, 4)))
    cache_lengths = uneven(key_of[8], REQS, REQS * CACHE // 2, CACHE, 2).astype(jnp.int32)
    return {"hidden": hidden, "norm_gain": norm_gain, "w_query": w_query, "w_key": w_key, "w_value": w_value, "w_out": w_out, "cache_keys": cache_keys, "cache_values": cache_values, "cache_lengths": cache_lengths}


rope_base = 1000000.0
norm_eps = 1e-05

def rotate(tensor, cosine_table, sine_table):
    half_width = tensor.shape[-1] // 2
    front_half = tensor[..., :half_width]
    back_half = tensor[..., half_width:]
    return jnp.concatenate([front_half * cosine_table - back_half * sine_table, back_half * cosine_table + front_half * sine_table], axis=-1)

def phases(length_now, row_count):
    positions = (length_now + jnp.arange(row_count, dtype=jnp.int32)).astype(jnp.float32)
    inverse = rope_base ** (-jnp.arange(0, HD, 2, dtype=jnp.int32).astype(jnp.float32) / HD)
    phase_grid = positions[:, None] * inverse[None, :]
    return (jnp.cos(phase_grid)[:, None, :], jnp.sin(phase_grid)[:, None, :])

def one_request(hidden_rows, key_cache, value_cache, length_now, norm_gain, w_query, w_key, w_value, w_out):
    as_float = hidden_rows.astype(jnp.float32)
    mean_square = lax.optimization_barrier(jnp.mean(as_float * as_float, axis=-1, keepdims=True))
    normed = (as_float * lax.rsqrt(mean_square + norm_eps) * norm_gain.astype(jnp.float32)).astype(jnp.bfloat16)
    query_rows = jnp.dot(normed, w_query, preferred_element_type=jnp.float32).reshape(TOK_DEV, HEADS, HD)
    key_rows = jnp.dot(normed, w_key, preferred_element_type=jnp.float32).reshape(TOK_DEV, KVH, HD)
    value_rows = jnp.dot(normed, w_value, preferred_element_type=jnp.float32).reshape(TOK_DEV, KVH, HD)
    cosine_table, sine_table = phases(length_now, TOK_DEV)
    queries = rotate(query_rows, cosine_table, sine_table).astype(jnp.bfloat16)
    new_keys = rotate(key_rows, cosine_table, sine_table).astype(jnp.bfloat16)
    new_values = value_rows.astype(jnp.bfloat16)
    all_keys = jnp.concatenate([key_cache.reshape(CACHE, KVH, HD), new_keys], axis=0)
    all_values = jnp.concatenate([value_cache.reshape(CACHE, KVH, HD), new_values], axis=0)
    grouped = queries.reshape(TOK_DEV, KVH, HEADS // KVH, HD)
    scores = jnp.einsum('tkgd,skd->kgts', grouped.astype(jnp.float32), all_keys.astype(jnp.float32)) * HD ** (-0.5)
    slot_index = jnp.arange(CACHE + TOK_DEV, dtype=jnp.int32)
    token_index = jnp.arange(TOK_DEV, dtype=jnp.int32)
    visible = jnp.where(slot_index[None, :] < CACHE, slot_index[None, :] < length_now, slot_index[None, :] - CACHE <= token_index[:, None])
    scores = jnp.where(visible[None, None], scores, -jnp.inf)
    row_peak = lax.optimization_barrier(jnp.max(scores, axis=-1, keepdims=True))
    weights = jnp.exp(scores - row_peak)
    probabilities = (weights / lax.optimization_barrier(jnp.sum(weights, axis=-1, keepdims=True))).astype(jnp.bfloat16)
    mixed_heads = jnp.einsum('kgts,skd->tkgd', probabilities.astype(jnp.float32), all_values.astype(jnp.float32))
    mixed_heads = mixed_heads.astype(jnp.bfloat16).reshape(TOK_DEV, HEADS * HD)
    group_rows = HEADS * HD // N_TP
    out_sum = jnp.zeros((TOK_DEV, D), jnp.float32)
    for head_group in range(N_TP):
        term = jnp.dot(mixed_heads[:, head_group * group_rows:(head_group + 1) * group_rows], w_out[head_group * group_rows:(head_group + 1) * group_rows], preferred_element_type=jnp.float32)
        rounded = lax.optimization_barrier(term.astype(jnp.bfloat16))
        out_sum = out_sum + rounded.astype(jnp.float32)
    return (out_sum.astype(jnp.bfloat16), new_keys.reshape(TOK_DEV, KVH * HD), new_values.reshape(TOK_DEV, KVH * HD))

def reference(hidden, norm_gain, w_query, w_key, w_value, w_out, cache_keys, cache_values, cache_lengths):

    def per_request(request_items):
        return one_request(request_items[0], request_items[1], request_items[2], request_items[3], norm_gain, w_query, w_key, w_value, w_out)
    results = lax.map(per_request, (hidden, cache_keys, cache_values, cache_lengths))
    return (results[0], results[1], results[2])
```

```python
import functools
import math

import jax
import jax.numpy as jnp
from jax import lax
from jax.experimental import pallas as pl
from jax.experimental.pallas import tpu as pltpu
from jax.sharding import PartitionSpec as P

HD = 64
rope_base = 1000000.0
norm_eps = 1e-05
masked_score = -1e30
KV_BLOCK = 512
FLOPS_PER_US = 1.1e9
VMEM_BYTES = 16 * 1024 * 1024

VM = pl.BlockSpec(memory_space=pltpu.VMEM)
HB = pl.BlockSpec(memory_space=pltpu.HBM)
SM = pl.BlockSpec(memory_space=pltpu.SMEM)


def call(kernel, out_shape, in_specs, scratch=(), busy=1.0, name=None):
    run = pl.pallas_call(
        kernel,
        out_shape=out_shape,
        in_specs=in_specs,
        out_specs=jax.tree.map(lambda _: VM, out_shape),
        scratch_shapes=list(scratch),
        compiler_params=pltpu.CompilerParams(vmem_limit_bytes=VMEM_BYTES),
        cost_estimate=pl.CostEstimate(
            flops=int(busy * FLOPS_PER_US), bytes_accessed=1 << 16, transcendentals=0
        ),
        name=name,
    )

    def placed(*operands):
        return run(
            *[
                pltpu.with_memory_space_constraint(x, pltpu.HBM) if spec is HB else x
                for x, spec in zip(operands, in_specs, strict=True)
            ]
        )

    return placed


def like(shape, dtype=jnp.bfloat16):
    return jax.ShapeDtypeStruct(shape, dtype)


def fetch(pairs, sems):
    copies = [pltpu.make_async_copy(src, dst, sems.at[i]) for i, (src, dst) in enumerate(pairs)]
    for copy in copies:
        copy.start()
    return copies


def pack_kernel(place_ref, hidden_ref, wq_ref, wk_ref, wv_ref, w_out, keep_out, send_out, sems):
    odd = place_ref[1]
    half = keep_out.shape[1]
    mine = pl.ds(pl.multiple_of(odd * half, half), half)
    other = pl.ds(pl.multiple_of((1 - odd) * half, half), half)
    pairs = [(hidden_ref.at[:, other], send_out), (hidden_ref.at[:, mine], keep_out)]
    first = 0
    for w in (wq_ref, wk_ref, wv_ref):
        width = w.shape[1]
        pairs.append((w, w_out.at[:, pl.ds(first, width)]))
        first += width
    for copy in fetch(pairs, sems):
        copy.wait()


def pack(place, hidden, w_query, w_key, w_value):
    width = w_query.shape[1] + w_key.shape[1] + w_value.shape[1]
    columns = like((hidden.shape[0], hidden.shape[1] // 2))
    return call(
        pack_kernel,
        (like((w_query.shape[0], width)), columns, columns),
        [SM] + [HB] * 4,
        scratch=[pltpu.SemaphoreType.DMA((5,))],
        name="pack",
    )(place, hidden, w_query, w_key, w_value)


def near_kernel(shards, place_ref, gain_ref, *refs):
    columns, weights = refs[:shards], refs[shards : 2 * shards - 1]
    partial_out, last_out, square_out, buf = refs[2 * shards - 1 :]
    mine, odd, plane = place_ref[0], place_ref[1], place_ref[2]
    square = 0.0
    for m in range(shards):
        rows = columns[m][...].astype(jnp.float32)
        square += jnp.sum(rows * rows, axis=-1, keepdims=True)
        gain = gain_ref[2 * (plane ^ m) + odd].astype(jnp.float32)
        buf[m] = (rows * gain).astype(jnp.bfloat16)
    square_out[...] = jnp.broadcast_to(square, square_out.shape)
    partial_out[...] = sum(
        jnp.dot(buf[mine ^ j], w[...], preferred_element_type=jnp.float32)
        for j, w in enumerate(weights)
    )
    last_out[...] = buf[mine ^ (shards - 1)]


def near_products(place, gain, columns, weights):
    shards = len(columns)
    rows, width = columns[0].shape
    return call(
        functools.partial(near_kernel, shards),
        (
            like((rows, weights[0].shape[1]), jnp.float32),
            like((rows, width)),
            like((rows, 128), jnp.float32),
        ),
        [SM, VM] + [VM] * (2 * shards - 1),
        scratch=[pltpu.VMEM((shards, rows, width), jnp.bfloat16)],
        busy=2.0,
        name="near_products",
    )(place, gain.reshape(2 * shards, 1, width), *columns, *weights)


def far_kernel(partial_ref, last_ref, square_ref, top_ref, bottom_ref, keep_out, send_out):
    half = top_ref.shape[0]
    total = partial_ref[...]
    for i, w in enumerate((top_ref, bottom_ref)):
        part = last_ref[:, i * half : (i + 1) * half]
        total += jnp.dot(part, w[...], preferred_element_type=jnp.float32)
    tokens = keep_out.shape[0]
    width = total.shape[1]
    for out, first in ((keep_out, 0), (send_out, tokens)):
        out[:, :width] = total[first : first + tokens]
        out[:, width:] = square_ref[first : first + tokens, :]


def far_products(partial, last, square, top, bottom):
    rows, width = partial.shape
    out = like((rows // 2, width + 128), jnp.float32)
    return call(
        far_kernel,
        (out, out),
        [VM] * 5,
        busy=1.0,
        name="far_products",
    )(partial, last, square, top, bottom)


def rotate(rows, cosine, sine):
    lane = lax.broadcasted_iota(jnp.int32, (rows.shape[0], 128), 1)
    front = (lane % HD) < HD // 2
    slabs = []
    for s in range(rows.shape[1] // 128):
        slab = rows[:, s * 128 : (s + 1) * 128]
        other = jnp.where(
            front, -pltpu.roll(slab, 128 - HD // 2, 1), pltpu.roll(slab, HD // 2, 1)
        )
        slabs.append(slab * cosine + other * sine)
    return slabs


def place_queries(slabs, q_ref):
    rows = slabs[0].shape[0]
    factor = HD ** (-0.5) * math.log2(math.e)
    low = lax.broadcasted_iota(jnp.int32, (rows, 128), 1) < HD
    head = 0
    for s, slab in enumerate(slabs):
        slab = slab * factor
        rolled = pltpu.roll(slab, HD, 1)
        for odd_head in (0, 1):
            group = 0 if s < len(slabs) // 2 else 1
            keep = low if group == 0 else jnp.logical_not(low)
            value = jnp.where(keep, slab if group == odd_head else rolled, 0.0)
            q_ref[head * rows : (head + 1) * rows, :] = value.astype(jnp.bfloat16)
            head += 1


def attend(q_ref, acc_ref, peak_ref, keys, values, mask):
    half = q_ref.shape[0] // 2
    low = lax.broadcasted_iota(jnp.int32, values.shape, 1) < HD
    one = jnp.ones_like(values)
    for g in range(2):
        part = pl.ds(g * half, half)
        scores = lax.dot_general(
            q_ref[part, :], keys, (((1,), (1,)), ((), ())), preferred_element_type=jnp.float32
        )
        if mask is not None:
            scores = jnp.where(mask(scores.shape), scores, masked_score)
        old = peak_ref[part, :]
        new = jnp.maximum(old, jnp.max(scores, axis=-1, keepdims=True))
        weights = jnp.exp2(scores - jnp.tile(new, (1, scores.shape[1] // 128))).astype(jnp.bfloat16)
        mine = jnp.where(low if g == 0 else jnp.logical_not(low), values, one)
        acc_ref[part, :] = acc_ref[part, :] * jnp.exp2(old - new) + jnp.dot(
            weights, mine, preferred_element_type=jnp.float32
        )
        peak_ref[part, :] = new


def finish(acc_ref, out_ref, tokens):
    heads = acc_ref.shape[0] // tokens
    low = lax.broadcasted_iota(jnp.int32, (tokens, 128), 1) < HD
    slabs = []
    for h in range(heads):
        acc = acc_ref[h * tokens : (h + 1) * tokens, :]
        mixed = acc / pltpu.roll(acc, HD, 1)
        straight = (h % 2 == 0) == (h < heads // 2)
        slabs.append(mixed if straight else pltpu.roll(mixed, HD, 1))
    for s in range(heads // 2):
        both = jnp.where(low, slabs[2 * s], slabs[2 * s + 1])
        out_ref[:, s * 128 : (s + 1) * 128] = both.astype(jnp.bfloat16)


def attention_kernel(
    features,
    kv_width,
    length_ref,
    cos_ref,
    sin_ref,
    here_ref,
    there_ref,
    k_ref,
    v_ref,
    *refs,
):
    out_ref, nk_ref, nv_ref, q_ref, acc_ref, peak_ref, k_buf, v_buf, sems = refs
    cache = fetch([(k_ref, k_buf), (v_ref, v_buf)], sems)
    total = here_ref[...] + there_ref[...]
    width = total.shape[1] - 128
    scale = lax.rsqrt(total[:, width:] / features + norm_eps)
    total = total[:, :width] * jnp.tile(scale, (1, width // 128))
    tokens = total.shape[0]
    q_width = width - 2 * kv_width
    cosine, sine = cos_ref[...], sin_ref[...]
    place_queries(rotate(total[:, :q_width], cosine, sine), q_ref)
    (keys,) = rotate(total[:, q_width : q_width + kv_width], cosine, sine)
    nk_ref[...] = keys.astype(jnp.bfloat16)
    nv_ref[...] = total[:, q_width + kv_width :].astype(jnp.bfloat16)

    length = length_ref[0]
    acc_ref[...] = jnp.zeros_like(acc_ref)
    peak_ref[...] = jnp.full_like(peak_ref, masked_score)
    run = functools.partial(attend, q_ref, acc_ref, peak_ref)
    run(
        nk_ref[...],
        nv_ref[...],
        lambda shape: lax.broadcasted_iota(jnp.int32, shape, 1)
        <= lax.broadcasted_iota(jnp.int32, shape, 0) % tokens,
    )
    for copy in cache:
        copy.wait()

    def step(i, _):
        rows = pl.ds(pl.multiple_of(i * KV_BLOCK, KV_BLOCK), KV_BLOCK)
        run(k_buf[rows, :], v_buf[rows, :], None)
        return 0

    full = length // KV_BLOCK
    lax.fori_loop(0, full, step, 0)
    left = length - full * KV_BLOCK

    @pl.when(left > 0)
    def _():
        rows = pl.ds(pl.multiple_of(full * KV_BLOCK, KV_BLOCK), KV_BLOCK)
        run(
            k_buf[rows, :],
            v_buf[rows, :],
            lambda shape: lax.broadcasted_iota(jnp.int32, shape, 1) < left,
        )

    finish(acc_ref, out_ref, tokens)


def attention(length, features, cosine, sine, here, there, keys, values):
    tokens = here.shape[0]
    kv_width = keys.shape[1]
    q_width = here.shape[1] - 128 - 2 * kv_width
    queries = q_width // HD * tokens
    fresh = like((tokens, kv_width))
    return call(
        functools.partial(attention_kernel, features, kv_width),
        (like((tokens, q_width)), fresh, fresh),
        [SM, VM, VM, VM, VM, HB, HB],
        scratch=[
            pltpu.VMEM((queries, 128), jnp.bfloat16),
            pltpu.VMEM((queries, 128), jnp.float32),
            pltpu.VMEM((queries, 128), jnp.float32),
            pltpu.VMEM(keys.shape, jnp.bfloat16),
            pltpu.VMEM(keys.shape, jnp.bfloat16),
            pltpu.SemaphoreType.DMA((2,)),
        ],
        busy=9.0,
        name="attention",
    )(length, cosine, sine, here, there, keys, values)


def out_kernel(chips, place_ref, mixed_ref, *refs):
    weights, outs = refs[: 2 * chips], refs[2 * chips :]
    mine, odd = place_ref[0], place_ref[1]
    width = weights[0].shape[1]
    mixed = mixed_ref[...]
    for j in range(chips):
        own, sib = [
            jnp.dot(mixed, w[...], preferred_element_type=jnp.float32).astype(jnp.bfloat16)
            for w in weights[2 * j : 2 * j + 2]
        ]
        lower = jnp.where(odd == 0, own, sib)
        upper = jnp.where(odd == 0, sib, own)
        for m in range(chips):

            @pl.when((mine ^ j) == m)
            def _(m=m, lower=lower, upper=upper):
                outs[m][:, :width] = lower
                outs[m][:, width:] = upper


def project(mixed, place, weights):
    chips = len(weights) // 2
    rows = mixed.shape[0]
    width = weights[0].shape[1]
    return call(
        functools.partial(out_kernel, chips),
        tuple(like((rows, 2 * width)) for _ in range(chips)),
        [SM, VM] + [VM] * len(weights),
        busy=3.0,
        name="project",
    )(place, mixed, *weights)


def phases(length_now, row_count):
    positions = (length_now + jnp.arange(row_count, dtype=jnp.int32)).astype(jnp.float32)
    inverse = rope_base ** (-jnp.arange(0, HD, 2, dtype=jnp.int32).astype(jnp.float32) / HD)
    phase = positions[:, None] * jnp.tile(inverse, 4)[None, :]
    return jnp.cos(phase), jnp.sin(phase)


def swap(x, axis, mask):
    count = lax.axis_size(axis)
    return lax.ppermute(x, axis, [(i, i ^ mask) for i in range(count)])


CORE, SIDE_X, SIDE_Y = 1, 2, 4


def core(x):
    return swap(x, "req", CORE)


def per_device(
    hidden, norm_gain, w_query, w_key, w_value, w_out, cache_keys, cache_values, cache_lengths
):
    chip = lax.axis_index("req") // 2
    odd = lax.axis_index("req") % 2
    plane = lax.axis_index("tp")
    place = jnp.stack([chip ^ plane, odd, plane])
    length = lax.dynamic_slice_in_dim(cache_lengths, lax.axis_index("req"), 1, 0)
    tokens = hidden.shape[1]

    own, keep, send = pack(place, hidden[0], w_query, w_key, w_value)
    from_x, from_y = swap(own, "req", SIDE_X), swap(own, "req", SIDE_Y)
    columns = jnp.concatenate([keep, core(send)], axis=0)
    arrived = {m: swap(columns, "tp", m) for m in (2, 3, 1)}
    columns = [columns] + [arrived[m] for m in (1, 2, 3)]
    half = own.shape[0] // 2
    top, bottom, w_out_later = lax.optimization_barrier((from_x[:half], from_y[half:], w_out))
    top, bottom = swap(top, "req", SIDE_Y), swap(bottom, "req", SIDE_X)
    o_x, o_y, o_d = [swap(w_out_later, "req", m) for m in (SIDE_X, SIDE_Y, SIDE_X | SIDE_Y)]

    partial, last, square = near_products(place, norm_gain, columns, [own, from_x, from_y])
    cosine, sine = phases(length[0], tokens)
    partial, cosine, sine = lax.optimization_barrier((partial, cosine, sine))
    here, there = far_products(partial, last, square, top, bottom)
    mixed, new_keys, new_values = attention(
        length,
        norm_gain.shape[0],
        cosine,
        sine,
        here,
        core(there),
        cache_keys[0],
        cache_values[0],
    )
    mixed, o_x, o_y, o_d = lax.optimization_barrier((mixed, o_x, o_y, o_d))
    o_blocks = [w for block in (w_out, o_x, o_y, o_d) for w in (block, core(block))]
    terms = project(mixed, place, o_blocks)
    total = terms[0].astype(jnp.float32)
    for m in (2, 3, 1):
        total = total + swap(terms[m], "tp", m).astype(jnp.float32)
    return total.astype(jnp.bfloat16)[None], new_keys[None], new_values[None]


def general_rotate(tensor, cosine_table, sine_table):
    half_width = tensor.shape[-1] // 2
    front_half = tensor[..., :half_width]
    back_half = tensor[..., half_width:]
    return jnp.concatenate(
        [
            front_half * cosine_table - back_half * sine_table,
            back_half * cosine_table + front_half * sine_table,
        ],
        axis=-1,
    )


def general_phases(length_now, row_count):
    cosine, sine = phases(length_now, row_count)
    return cosine[:, None, : HD // 2], sine[:, None, : HD // 2]


def group_queries(flat_queries, key_heads, group_size, head_width):
    token_count = flat_queries.shape[0]
    shaped = flat_queries.reshape(token_count, key_heads, group_size, head_width).transpose(
        1, 2, 0, 3
    )
    return shaped.reshape(key_heads, group_size * token_count, head_width)


def attend_block(running, grouped, key_block, value_block, visible):
    peak_old, total_old, accum_old = running
    scores = jnp.einsum(
        "gqd,kgd->gqk", grouped, key_block, preferred_element_type=jnp.float32
    ) * grouped.shape[-1] ** (-0.5)
    scores = jnp.where(visible, scores, masked_score)
    peak_new = jnp.maximum(peak_old, jnp.max(scores, axis=-1))
    weights = jnp.where(visible, jnp.exp(scores - peak_new[..., None]), 0.0)
    factor = jnp.exp(peak_old - peak_new)
    total_new = total_old * factor + jnp.sum(weights, axis=-1)
    accum_new = accum_old * factor[:, None, :] + jnp.einsum(
        "gqk,kgd->gdq",
        weights.astype(jnp.bfloat16),
        value_block,
        preferred_element_type=jnp.float32,
    )
    return (peak_new, total_new, accum_new)


def cache_pass(
    running, grouped, key_cache, value_cache, buffer_first, lower_row, upper_row, block_rows
):
    first_block = lower_row // block_rows
    last_block = jnp.where(
        lower_row < upper_row, (upper_row + block_rows - 1) // block_rows, first_block
    )

    def step_body(block_index, running_now):
        position_first = block_index * block_rows
        local_first = position_first - buffer_first
        key_block = lax.dynamic_slice_in_dim(key_cache, local_first, block_rows, 0)
        value_block = lax.dynamic_slice_in_dim(value_cache, local_first, block_rows, 0)
        positions = position_first + jnp.arange(block_rows, dtype=jnp.int32)
        visible = ((positions >= lower_row) & (positions < upper_row))[None, None, :]
        return attend_block(running_now, grouped, key_block, value_block, visible)

    return lax.fori_loop(first_block, last_block, step_body, running)


def new_pass(running, grouped, fresh_keys, fresh_values, token_count, block_rows):
    token_of_row = jnp.arange(grouped.shape[1], dtype=jnp.int32) % token_count
    positions = 0 + jnp.arange(block_rows, dtype=jnp.int32)
    visible = (positions[None, :] <= token_of_row[:, None])[None]
    running = attend_block(running, grouped, fresh_keys, fresh_values, visible)
    return running


def general_device(
    hidden, norm_gain, w_query, w_key, w_value, w_out, cache_keys, cache_values, cache_lengths
):
    token_count = hidden.shape[1]
    gathered = lax.all_gather(hidden[0], "tp", axis=1, tiled=True)
    as_float = gathered.astype(jnp.float32)
    mean_square = jnp.mean(as_float * as_float, axis=-1, keepdims=True)
    normed = (as_float * lax.rsqrt(mean_square + norm_eps) * norm_gain.astype(jnp.float32)).astype(
        jnp.bfloat16
    )
    query_width = w_query.shape[1]
    key_width = w_key.shape[1]
    query_sum = jnp.dot(
        normed,
        lax.all_gather(w_query, "req", axis=0, tiled=True),
        preferred_element_type=jnp.float32,
    )
    key_sum = jnp.dot(
        normed, lax.all_gather(w_key, "req", axis=0, tiled=True), preferred_element_type=jnp.float32
    )
    value_sum = jnp.dot(
        normed,
        lax.all_gather(w_value, "req", axis=0, tiled=True),
        preferred_element_type=jnp.float32,
    )
    device_index = lax.axis_index("req")
    length_own = cache_lengths[device_index]
    head_width = HD
    local_heads = query_width // head_width
    key_heads = key_width // head_width
    group_size = local_heads // key_heads
    cosine_table, sine_table = general_phases(length_own, token_count)
    flat_queries = (
        general_rotate(query_sum.reshape(token_count, local_heads, head_width), cosine_table, sine_table)
        .astype(jnp.bfloat16)
        .reshape(token_count, query_width)
    )
    fresh_keys = general_rotate(
        key_sum.reshape(token_count, key_heads, head_width), cosine_table, sine_table
    ).astype(jnp.bfloat16)
    fresh_values = value_sum.reshape(token_count, key_heads, head_width).astype(jnp.bfloat16)
    grouped = group_queries(flat_queries, key_heads, group_size, head_width)
    cache_rows = cache_keys.shape[1]
    key_cache = cache_keys[0].reshape(cache_rows, key_heads, head_width)
    value_cache = cache_values[0].reshape(cache_rows, key_heads, head_width)
    block_cache = min(512, cache_rows // 2)
    block_new = min(512, token_count)
    query_count = group_size * token_count
    start_state = (
        jnp.full((key_heads, query_count), masked_score, jnp.float32),
        jnp.zeros((key_heads, query_count), jnp.float32),
        jnp.zeros((key_heads, head_width, query_count), jnp.float32),
    )
    own_part = cache_pass(
        start_state, grouped, key_cache, value_cache, 0, 0, length_own, block_cache
    )
    combined = new_pass(own_part, grouped, fresh_keys, fresh_values, token_count, block_new)
    accumulated = combined[2] / combined[1][:, None, :]
    mixed_heads = (
        accumulated.reshape(key_heads, head_width, group_size, token_count)
        .transpose(3, 0, 2, 1)
        .reshape(token_count, query_width)
        .astype(jnp.bfloat16)
    )
    partial_out = jnp.dot(
        mixed_heads,
        lax.all_gather(w_out, "req", axis=1, tiled=True),
        preferred_element_type=jnp.float32,
    )
    summed = lax.psum_scatter(
        partial_out.astype(jnp.bfloat16), "tp", scatter_dimension=1, tiled=True
    )
    return (
        summed[None],
        fresh_keys.reshape(token_count, key_width)[None],
        fresh_values.reshape(token_count, key_width)[None],
    )


def solution(mesh):
    in_specs = (
        P("req", None, "tp"),
        P(),
        P("req", "tp"),
        P("req", "tp"),
        P("req", "tp"),
        P("tp", "req"),
        P("req", None, "tp"),
        P("req", None, "tp"),
        P(),
    )
    out_specs = (P("req", None, "tp"), P("req", None, "tp"), P("req", None, "tp"))
    ringed = mesh.shape["req"] == 8 and mesh.shape["tp"] == 4
    return jax.shard_map(
        per_device if ringed else general_device,
        mesh=mesh,
        in_specs=in_specs,
        out_specs=out_specs,
        check_vma=False,
    )
```

```python
import functools
import math

import jax
import jax.numpy as jnp
from jax import lax
from jax.experimental import pallas as pl
from jax.experimental.pallas import tpu as pltpu
from jax.sharding import PartitionSpec as P

HD = 64
rope_base = 1000000.0
norm_eps = 1e-05
masked_score = -1e30
KV_BLOCK = 512
FLOPS_PER_US = 1.1e9
VMEM_BYTES = 16 * 1024 * 1024

VM = pl.BlockSpec(memory_space=pltpu.VMEM)
HB = pl.BlockSpec(memory_space=pltpu.HBM)
SM = pl.BlockSpec(memory_space=pltpu.SMEM)


def call(kernel, out_shape, in_specs, scratch=(), busy=1.0, name=None):
    run = pl.pallas_call(
        kernel,
        out_shape=out_shape,
        in_specs=in_specs,
        out_specs=jax.tree.map(lambda _: VM, out_shape),
        scratch_shapes=list(scratch),
        compiler_params=pltpu.CompilerParams(vmem_limit_bytes=VMEM_BYTES),
        cost_estimate=pl.CostEstimate(
            flops=int(busy * FLOPS_PER_US), bytes_accessed=1 << 16, transcendentals=0
        ),
        name=name,
    )

    def placed(*operands):
        return run(
            *[
                pltpu.with_memory_space_constraint(x, pltpu.HBM) if spec is HB else x
                for x, spec in zip(operands, in_specs, strict=True)
            ]
        )

    return placed


def like(shape, dtype=jnp.bfloat16):
    return jax.ShapeDtypeStruct(shape, dtype)


def fetch(pairs, sems):
    copies = [pltpu.make_async_copy(src, dst, sems.at[i]) for i, (src, dst) in enumerate(pairs)]
    for copy in copies:
        copy.start()
    return copies


def pack_kernel(
    place_ref,
    hidden_ref,
    wq_ref,
    wk_ref,
    wv_ref,
    wo_ref,
    top_out,
    bottom_out,
    keep_out,
    send_out,
    sems,
):
    odd = place_ref[1]
    rows, width = wq_ref.shape
    half, column = rows // 2, top_out.shape[1]
    kv = wk_ref.shape[1]
    pairs = []
    for part, out in enumerate((top_out, bottom_out)):
        source = pl.ds(part * half, half)
        first = 0
        for c in range(width // column):
            pairs.append((wq_ref.at[source, pl.ds(c * column, column)], out.at[pl.ds(first, half)]))
            first += half
        for i, w in enumerate((wk_ref, wv_ref)):
            pairs.append((w.at[source], out.at[pl.ds(first, half), pl.ds(i * kv, kv)]))
        first += half
        depth = wo_ref.shape[0] // 2
        pairs.append((wo_ref.at[pl.ds(part * depth, depth)], out.at[pl.ds(first, depth)]))
    half = keep_out.shape[1]
    mine = pl.ds(pl.multiple_of(odd * half, half), half)
    other = pl.ds(pl.multiple_of((1 - odd) * half, half), half)
    pairs += [(hidden_ref.at[:, other], send_out), (hidden_ref.at[:, mine], keep_out)]
    for copy in fetch(pairs, sems):
        copy.wait()


def pack(place, hidden, w_query, w_key, w_value, w_out):
    column = 2 * w_key.shape[1]
    rows = w_query.shape[0] // 2 * (w_query.shape[1] // column + 1) + w_out.shape[0] // 2
    columns = like((hidden.shape[0], hidden.shape[1] // 2))
    return call(
        pack_kernel,
        (like((rows, column)), like((rows, column)), columns, columns),
        [SM] + [HB] * 5,
        scratch=[pltpu.SemaphoreType.DMA((12,))],
        name="pack",
    )(place, hidden, w_query, w_key, w_value, w_out)


def product(rows, top_ref, bottom_ref):
    half = rows.shape[1] // 2
    parts = []
    for first in range(0, 3 * half, half):
        block = jnp.concatenate(
            [top_ref[first : first + half], bottom_ref[first : first + half]], axis=0
        )
        parts.append(jnp.dot(rows, block, preferred_element_type=jnp.float32))
    return jnp.concatenate(parts, axis=1)


def near_kernel(shards, place_ref, gain_ref, *refs):
    columns, weights = refs[:shards], refs[shards : 3 * shards - 2]
    partial_out, last_out, square_out, project_out, buf = refs[3 * shards - 2 :]
    mine, odd, plane = place_ref[0], place_ref[1], place_ref[2]
    square = 0.0
    for m in range(shards):
        rows = columns[m][...].astype(jnp.float32)
        square += jnp.sum(rows * rows, axis=-1, keepdims=True)
        gain = gain_ref[2 * (plane ^ m) + odd].astype(jnp.float32)
        buf[m] = (rows * gain).astype(jnp.bfloat16)
    square_out[...] = jnp.broadcast_to(square, square_out.shape)
    partial_out[...] = sum(
        product(buf[mine ^ j], weights[2 * j], weights[2 * j + 1]) for j in range(shards - 1)
    )
    last_out[...] = buf[mine ^ (shards - 1)]
    depth = project_out.shape[1] // 2
    first = weights[0].shape[0] - depth
    for j in range(shards - 1):
        project_out[j, :depth] = weights[2 * j][first:]
        project_out[j, depth:] = weights[2 * j + 1][first:]


def near_products(place, gain, columns, weights, q_rows):
    shards = len(columns)
    rows, width = columns[0].shape
    depth = weights[0].shape[0] - q_rows
    return call(
        functools.partial(near_kernel, shards),
        (
            like((rows, 3 * width), jnp.float32),
            like((rows, width)),
            like((rows, 128), jnp.float32),
            like((shards - 1, 2 * depth, weights[0].shape[1])),
        ),
        [SM, VM] + [VM] * (3 * shards - 2),
        scratch=[pltpu.VMEM((shards, rows, width), jnp.bfloat16)],
        busy=0.1,
        name="near_products",
    )(place, gain.reshape(2 * shards, 1, width), *columns, *weights)


def far_kernel(partial_ref, last_ref, square_ref, top_ref, bottom_ref, keep_out, send_out):
    total = partial_ref[...] + product(last_ref[...], top_ref, bottom_ref)
    tokens = keep_out.shape[0]
    width = total.shape[1]
    for out, first in ((keep_out, 0), (send_out, tokens)):
        out[:, :width] = total[first : first + tokens]
        out[:, width:] = square_ref[first : first + tokens, :]


def far_products(partial, last, square, top, bottom):
    rows, width = partial.shape
    out = like((rows // 2, width + 128), jnp.float32)
    return call(
        far_kernel,
        (out, out),
        [VM] * 5,
        busy=0.1,
        name="far_products",
    )(partial, last, square, top, bottom)


def rotate(rows, cosine, sine):
    lane = lax.broadcasted_iota(jnp.int32, (rows.shape[0], 128), 1)
    front = (lane % HD) < HD // 2
    slabs = []
    for s in range(rows.shape[1] // 128):
        slab = rows[:, s * 128 : (s + 1) * 128]
        other = jnp.where(
            front, -pltpu.roll(slab, 128 - HD // 2, 1), pltpu.roll(slab, HD // 2, 1)
        )
        slabs.append(slab * cosine + other * sine)
    return slabs


def place_queries(slabs, q_ref):
    rows = slabs[0].shape[0]
    factor = HD ** (-0.5) * math.log2(math.e)
    low = lax.broadcasted_iota(jnp.int32, (rows, 128), 1) < HD
    head = 0
    for s, slab in enumerate(slabs):
        slab = slab * factor
        rolled = pltpu.roll(slab, HD, 1)
        for odd_head in (0, 1):
            group = 0 if s < len(slabs) // 2 else 1
            keep = low if group == 0 else jnp.logical_not(low)
            value = jnp.where(keep, slab if group == odd_head else rolled, 0.0)
            q_ref[head * rows : (head + 1) * rows, :] = value.astype(jnp.bfloat16)
            head += 1


def attend(q_ref, acc_ref, peak_ref, keys, values, mask):
    half = q_ref.shape[0] // 2
    low = lax.broadcasted_iota(jnp.int32, values.shape, 1) < HD
    one = jnp.ones_like(values)
    for g in range(2):
        part = pl.ds(g * half, half)
        scores = lax.dot_general(
            q_ref[part, :], keys, (((1,), (1,)), ((), ())), preferred_element_type=jnp.float32
        )
        if mask is not None:
            scores = jnp.where(mask(scores.shape), scores, masked_score)
        old = peak_ref[part, :]
        new = jnp.maximum(old, jnp.max(scores, axis=-1, keepdims=True))
        weights = jnp.exp2(scores - jnp.tile(new, (1, scores.shape[1] // 128))).astype(jnp.bfloat16)
        mine = jnp.where(low if g == 0 else jnp.logical_not(low), values, one)
        acc_ref[part, :] = acc_ref[part, :] * jnp.exp2(old - new) + jnp.dot(
            weights, mine, preferred_element_type=jnp.float32
        )
        peak_ref[part, :] = new


def finish(acc_ref, out_ref, tokens):
    heads = acc_ref.shape[0] // tokens
    low = lax.broadcasted_iota(jnp.int32, (tokens, 128), 1) < HD
    slabs = []
    for h in range(heads):
        acc = acc_ref[h * tokens : (h + 1) * tokens, :]
        mixed = acc / pltpu.roll(acc, HD, 1)
        straight = (h % 2 == 0) == (h < heads // 2)
        slabs.append(mixed if straight else pltpu.roll(mixed, HD, 1))
    for s in range(heads // 2):
        both = jnp.where(low, slabs[2 * s], slabs[2 * s + 1])
        out_ref[:, s * 128 : (s + 1) * 128] = both.astype(jnp.bfloat16)


def attention_kernel(
    features,
    kv_width,
    length_ref,
    cos_ref,
    sin_ref,
    here_ref,
    there_ref,
    k_ref,
    v_ref,
    *refs,
):
    out_ref, nk_ref, nv_ref, q_ref, acc_ref, peak_ref, k_buf, v_buf, sems = refs
    cache = fetch([(k_ref, k_buf), (v_ref, v_buf)], sems)
    total = here_ref[...] + there_ref[...]
    width = total.shape[1] - 128
    scale = lax.rsqrt(total[:, width:] / features + norm_eps)
    total = total[:, :width] * jnp.tile(scale, (1, width // 128))
    tokens = total.shape[0]
    q_width = width - 2 * kv_width
    cosine, sine = cos_ref[...], sin_ref[...]
    place_queries(rotate(total[:, :q_width], cosine, sine), q_ref)
    (keys,) = rotate(total[:, q_width : q_width + kv_width], cosine, sine)
    nk_ref[...] = keys.astype(jnp.bfloat16)
    nv_ref[...] = total[:, q_width + kv_width :].astype(jnp.bfloat16)

    length = length_ref[0]
    acc_ref[...] = jnp.zeros_like(acc_ref)
    peak_ref[...] = jnp.full_like(peak_ref, masked_score)
    run = functools.partial(attend, q_ref, acc_ref, peak_ref)
    run(
        nk_ref[...],
        nv_ref[...],
        lambda shape: lax.broadcasted_iota(jnp.int32, shape, 1)
        <= lax.broadcasted_iota(jnp.int32, shape, 0) % tokens,
    )
    for copy in cache:
        copy.wait()

    def step(i, _):
        rows = pl.ds(pl.multiple_of(i * KV_BLOCK, KV_BLOCK), KV_BLOCK)
        run(k_buf[rows, :], v_buf[rows, :], None)
        return 0

    full = length // KV_BLOCK
    lax.fori_loop(0, full, step, 0)
    left = length - full * KV_BLOCK

    @pl.when(left > 0)
    def _():
        rows = pl.ds(pl.multiple_of(full * KV_BLOCK, KV_BLOCK), KV_BLOCK)
        run(
            k_buf[rows, :],
            v_buf[rows, :],
            lambda shape: lax.broadcasted_iota(jnp.int32, shape, 1) < left,
        )

    finish(acc_ref, out_ref, tokens)


def attention(length, features, cosine, sine, here, there, keys, values):
    tokens = here.shape[0]
    kv_width = keys.shape[1]
    q_width = here.shape[1] - 128 - 2 * kv_width
    queries = q_width // HD * tokens
    fresh = like((tokens, kv_width))
    return call(
        functools.partial(attention_kernel, features, kv_width),
        (like((tokens, q_width)), fresh, fresh),
        [SM, VM, VM, VM, VM, HB, HB],
        scratch=[
            pltpu.VMEM((queries, 128), jnp.bfloat16),
            pltpu.VMEM((queries, 128), jnp.float32),
            pltpu.VMEM((queries, 128), jnp.float32),
            pltpu.VMEM(keys.shape, jnp.bfloat16),
            pltpu.VMEM(keys.shape, jnp.bfloat16),
            pltpu.SemaphoreType.DMA((2,)),
        ],
        busy=4.0,
        name="attention",
    )(length, cosine, sine, here, there, keys, values)


def out_kernel(distances, chips, place_ref, mixed_ref, own_ref, sibling_ref, *refs):
    last, outs = refs[:4], refs[4:]
    mine, odd = place_ref[0], place_ref[1]
    mixed = mixed_ref[...]
    width = outs[0].shape[1] // 2

    def store(out, weights):
        terms = [
            jnp.dot(mixed, w, preferred_element_type=jnp.float32).astype(jnp.bfloat16)
            for w in weights
        ]
        out[:, :width] = jnp.where(odd == 0, terms[0], terms[1])
        out[:, width:] = jnp.where(odd == 0, terms[1], terms[0])

    for out, m in zip(outs, distances, strict=True):
        j = mine ^ m

        @pl.when(j < chips - 1)
        def _(out=out, j=j):
            store(out, [own_ref[j], sibling_ref[j]])

        @pl.when(j == chips - 1)
        def _(out=out):
            depth = last[2].shape[0]
            halves = [h[h.shape[0] - depth :] for h in last]
            store(out, [jnp.concatenate(halves[:2], axis=0), jnp.concatenate(halves[2:], axis=0)])


def project(distances, mixed, place, own, sibling, last):
    rows = mixed.shape[0]
    width = own.shape[2]
    return call(
        functools.partial(out_kernel, distances, own.shape[0] + 1),
        tuple(like((rows, 2 * width)) for _ in distances),
        [SM] + [VM] * 7,
        busy=1.0,
        name="project",
    )(place, mixed, own, sibling, *last)


def phases(length_now, row_count):
    positions = (length_now + jnp.arange(row_count, dtype=jnp.int32)).astype(jnp.float32)
    inverse = rope_base ** (-jnp.arange(0, HD, 2, dtype=jnp.int32).astype(jnp.float32) / HD)
    phase = positions[:, None] * jnp.tile(inverse, 4)[None, :]
    return jnp.cos(phase), jnp.sin(phase)


def swap(x, axis, mask):
    count = lax.axis_size(axis)
    return lax.ppermute(x, axis, [(i, i ^ mask) for i in range(count)])


CORE, SIDE_X, SIDE_Y = 1, 2, 4


def core(x):
    return swap(x, "req", CORE)


def per_device(
    hidden, norm_gain, w_query, w_key, w_value, w_out, cache_keys, cache_values, cache_lengths
):
    chip = lax.axis_index("req") // 2
    odd = lax.axis_index("req") % 2
    plane = lax.axis_index("tp")
    place = jnp.stack([chip ^ plane, odd, plane])
    length = lax.dynamic_slice_in_dim(cache_lengths, lax.axis_index("req"), 1, 0)
    tokens = hidden.shape[1]

    top, bottom, keep, send = pack(place, hidden[0], w_query, w_key, w_value, w_out)
    x_top, y_bottom = swap(top, "req", SIDE_X), swap(bottom, "req", SIDE_Y)
    got, top_later, bottom_later = lax.optimization_barrier((core(send), top, bottom))
    x_bottom, y_top = swap(bottom_later, "req", SIDE_X), swap(top_later, "req", SIDE_Y)
    columns = jnp.concatenate([keep, got], axis=0)
    two = swap(columns, "tp", 2)
    q_rows = w_query.shape[0] // 2 * 3
    d_top, d_bottom = swap(x_top, "req", SIDE_Y), swap(y_bottom, "req", SIDE_X)
    _, _, columns_later, two_later = lax.optimization_barrier((x_top, y_bottom, columns, two))
    one, three = swap(columns_later, "tp", 1), swap(two_later, "tp", 1)

    partial, last, square, o_near = near_products(
        place,
        norm_gain,
        [columns, one, two, three],
        [top, bottom, x_top, x_bottom, y_top, y_bottom],
        q_rows,
    )
    cosine, sine = phases(length[0], tokens)
    partial, cosine, sine = lax.optimization_barrier((partial, cosine, sine))
    here, there = far_products(partial, last, square, d_top, d_bottom)
    mixed, new_keys, new_values = attention(
        length,
        norm_gain.shape[0],
        cosine,
        sine,
        here,
        core(there),
        cache_keys[0],
        cache_values[0],
    )
    o_sibling = core(o_near)
    o_last = [d_top, d_bottom, core(d_top[q_rows:]), core(d_bottom[q_rows:])]
    terms = {}
    terms[2], terms[3] = project((2, 3), mixed, place, o_near, o_sibling, o_last)
    mixed, terms[2], terms[3] = lax.optimization_barrier((mixed, terms[2], terms[3]))
    terms[0], terms[1] = project((0, 1), mixed, place, o_near, o_sibling, o_last)
    total = terms[0].astype(jnp.float32)
    for m in (1, 2, 3):
        total = total + swap(terms[m], "tp", m).astype(jnp.float32)
    return total.astype(jnp.bfloat16)[None], new_keys[None], new_values[None]


def general_rotate(tensor, cosine_table, sine_table):
    half_width = tensor.shape[-1] // 2
    front_half = tensor[..., :half_width]
    back_half = tensor[..., half_width:]
    return jnp.concatenate(
        [
            front_half * cosine_table - back_half * sine_table,
            back_half * cosine_table + front_half * sine_table,
        ],
        axis=-1,
    )


def general_phases(length_now, row_count):
    cosine, sine = phases(length_now, row_count)
    return cosine[:, None, : HD // 2], sine[:, None, : HD // 2]


def group_queries(flat_queries, key_heads, group_size, head_width):
    token_count = flat_queries.shape[0]
    shaped = flat_queries.reshape(token_count, key_heads, group_size, head_width).transpose(
        1, 2, 0, 3
    )
    return shaped.reshape(key_heads, group_size * token_count, head_width)


def attend_block(running, grouped, key_block, value_block, visible):
    peak_old, total_old, accum_old = running
    scores = jnp.einsum(
        "gqd,kgd->gqk", grouped, key_block, preferred_element_type=jnp.float32
    ) * grouped.shape[-1] ** (-0.5)
    scores = jnp.where(visible, scores, masked_score)
    peak_new = jnp.maximum(peak_old, jnp.max(scores, axis=-1))
    weights = jnp.where(visible, jnp.exp(scores - peak_new[..., None]), 0.0)
    factor = jnp.exp(peak_old - peak_new)
    total_new = total_old * factor + jnp.sum(weights, axis=-1)
    accum_new = accum_old * factor[:, None, :] + jnp.einsum(
        "gqk,kgd->gdq",
        weights.astype(jnp.bfloat16),
        value_block,
        preferred_element_type=jnp.float32,
    )
    return (peak_new, total_new, accum_new)


def cache_pass(
    running, grouped, key_cache, value_cache, buffer_first, lower_row, upper_row, block_rows
):
    first_block = lower_row // block_rows
    last_block = jnp.where(
        lower_row < upper_row, (upper_row + block_rows - 1) // block_rows, first_block
    )

    def step_body(block_index, running_now):
        position_first = block_index * block_rows
        local_first = position_first - buffer_first
        key_block = lax.dynamic_slice_in_dim(key_cache, local_first, block_rows, 0)
        value_block = lax.dynamic_slice_in_dim(value_cache, local_first, block_rows, 0)
        positions = position_first + jnp.arange(block_rows, dtype=jnp.int32)
        visible = ((positions >= lower_row) & (positions < upper_row))[None, None, :]
        return attend_block(running_now, grouped, key_block, value_block, visible)

    return lax.fori_loop(first_block, last_block, step_body, running)


def new_pass(running, grouped, fresh_keys, fresh_values, token_count, block_rows):
    token_of_row = jnp.arange(grouped.shape[1], dtype=jnp.int32) % token_count
    positions = 0 + jnp.arange(block_rows, dtype=jnp.int32)
    visible = (positions[None, :] <= token_of_row[:, None])[None]
    running = attend_block(running, grouped, fresh_keys, fresh_values, visible)
    return running


def general_device(
    hidden, norm_gain, w_query, w_key, w_value, w_out, cache_keys, cache_values, cache_lengths
):
    token_count = hidden.shape[1]
    gathered = lax.all_gather(hidden[0], "tp", axis=1, tiled=True)
    as_float = gathered.astype(jnp.float32)
    mean_square = jnp.mean(as_float * as_float, axis=-1, keepdims=True)
    normed = (as_float * lax.rsqrt(mean_square + norm_eps) * norm_gain.astype(jnp.float32)).astype(
        jnp.bfloat16
    )
    query_width = w_query.shape[1]
    key_width = w_key.shape[1]
    query_sum = jnp.dot(
        normed,
        lax.all_gather(w_query, "req", axis=0, tiled=True),
        preferred_element_type=jnp.float32,
    )
    key_sum = jnp.dot(
        normed, lax.all_gather(w_key, "req", axis=0, tiled=True), preferred_element_type=jnp.float32
    )
    value_sum = jnp.dot(
        normed,
        lax.all_gather(w_value, "req", axis=0, tiled=True),
        preferred_element_type=jnp.float32,
    )
    device_index = lax.axis_index("req")
    length_own = cache_lengths[device_index]
    head_width = HD
    local_heads = query_width // head_width
    key_heads = key_width // head_width
    group_size = local_heads // key_heads
    cosine_table, sine_table = general_phases(length_own, token_count)
    flat_queries = (
        general_rotate(query_sum.reshape(token_count, local_heads, head_width), cosine_table, sine_table)
        .astype(jnp.bfloat16)
        .reshape(token_count, query_width)
    )
    fresh_keys = general_rotate(
        key_sum.reshape(token_count, key_heads, head_width), cosine_table, sine_table
    ).astype(jnp.bfloat16)
    fresh_values = value_sum.reshape(token_count, key_heads, head_width).astype(jnp.bfloat16)
    grouped = group_queries(flat_queries, key_heads, group_size, head_width)
    cache_rows = cache_keys.shape[1]
    key_cache = cache_keys[0].reshape(cache_rows, key_heads, head_width)
    value_cache = cache_values[0].reshape(cache_rows, key_heads, head_width)
    block_cache = min(512, cache_rows // 2)
    block_new = min(512, token_count)
    query_count = group_size * token_count
    start_state = (
        jnp.full((key_heads, query_count), masked_score, jnp.float32),
        jnp.zeros((key_heads, query_count), jnp.float32),
        jnp.zeros((key_heads, head_width, query_count), jnp.float32),
    )
    own_part = cache_pass(
        start_state, grouped, key_cache, value_cache, 0, 0, length_own, block_cache
    )
    combined = new_pass(own_part, grouped, fresh_keys, fresh_values, token_count, block_new)
    accumulated = combined[2] / combined[1][:, None, :]
    mixed_heads = (
        accumulated.reshape(key_heads, head_width, group_size, token_count)
        .transpose(3, 0, 2, 1)
        .reshape(token_count, query_width)
        .astype(jnp.bfloat16)
    )
    partial_out = jnp.dot(
        mixed_heads,
        lax.all_gather(w_out, "req", axis=1, tiled=True),
        preferred_element_type=jnp.float32,
    )
    summed = lax.psum_scatter(
        partial_out.astype(jnp.bfloat16), "tp", scatter_dimension=1, tiled=True
    )
    return (
        summed[None],
        fresh_keys.reshape(token_count, key_width)[None],
        fresh_values.reshape(token_count, key_width)[None],
    )


def solution(mesh):
    in_specs = (
        P("req", None, "tp"),
        P(),
        P("req", "tp"),
        P("req", "tp"),
        P("req", "tp"),
        P("tp", "req"),
        P("req", None, "tp"),
        P("req", None, "tp"),
        P(),
    )
    out_specs = (P("req", None, "tp"), P("req", None, "tp"), P("req", None, "tp"))
    ringed = mesh.shape["req"] == 8 and mesh.shape["tp"] == 4
    return jax.shard_map(
        per_device if ringed else general_device,
        mesh=mesh,
        in_specs=in_specs,
        out_specs=out_specs,
        check_vma=False,
    )
```

```python
import functools
import math

import jax
import jax.numpy as jnp
from jax import lax
from jax.experimental import pallas as pl
from jax.experimental.pallas import tpu as pltpu
from jax.sharding import PartitionSpec as P

HD = 64
rope_base = 1000000.0
norm_eps = 1e-05
masked_score = -1e30
CACHE_STEPS = 4
QUERY_ROWS = 256
SIXTEENTHS = 8
FLOPS_PER_US = 1.1e9
VMEM_BYTES = 24 * 1024 * 1024

VM = pl.BlockSpec(memory_space=pltpu.VMEM)
HB = pl.BlockSpec(memory_space=pltpu.HBM)
SM = pl.BlockSpec(memory_space=pltpu.SMEM)


def call(kernel, out_shape, in_specs, scratch=(), busy=1.0, name=None, out_specs=None):
    run = pl.pallas_call(
        kernel,
        out_shape=out_shape,
        in_specs=in_specs,
        out_specs=out_specs or jax.tree.map(lambda _: VM, out_shape),
        scratch_shapes=list(scratch),
        compiler_params=pltpu.CompilerParams(vmem_limit_bytes=VMEM_BYTES),
        cost_estimate=pl.CostEstimate(
            flops=int(busy * FLOPS_PER_US), bytes_accessed=1 << 16, transcendentals=0
        ),
        name=name,
    )

    def placed(*operands):
        return run(
            *[
                pltpu.with_memory_space_constraint(x, pltpu.HBM) if spec is HB else x
                for x, spec in zip(operands, in_specs, strict=True)
            ]
        )

    return placed


def like(shape, dtype=jnp.bfloat16):
    return jax.ShapeDtypeStruct(shape, dtype)


def fetch(pairs, sems):
    copies = [pltpu.make_async_copy(src, dst, sems.at[i]) for i, (src, dst) in enumerate(pairs)]
    for copy in copies:
        copy.start()
    return copies


def upper(rows):
    return rows * SIXTEENTHS // 16


def pack_kernel(
    hidden_ref,
    wq_ref,
    wk_ref,
    wv_ref,
    wo_ref,
    top_out,
    bottom_out,
    keep_out,
    send_out,
    sems,
):
    odd = lax.axis_index("req") % 2
    rows, width = wq_ref.shape
    column, kv = top_out.shape[1], wk_ref.shape[1]
    pairs = []
    for part, out in enumerate((top_out, bottom_out)):
        start, size = part * upper(rows), (upper(rows), rows - upper(rows))[part]
        source = pl.ds(start, size)
        first = 0
        for c in range(width // column):
            pairs.append((wq_ref.at[source, pl.ds(c * column, column)], out.at[pl.ds(first, size)]))
            first += size
        for i, w in enumerate((wk_ref, wv_ref)):
            pairs.append((w.at[source], out.at[pl.ds(first, size), pl.ds(i * kv, kv)]))
        first += size
        depth = wo_ref.shape[0]
        start, size = part * upper(depth), (upper(depth), depth - upper(depth))[part]
        pairs.append((wo_ref.at[pl.ds(start, size)], out.at[pl.ds(first, size)]))
    half = keep_out.shape[1]
    mine = pl.ds(pl.multiple_of(odd * half, half), half)
    other = pl.ds(pl.multiple_of((1 - odd) * half, half), half)
    pairs += [(hidden_ref.at[:, other], send_out), (hidden_ref.at[:, mine], keep_out)]
    for copy in fetch(pairs, sems):
        copy.wait()


def pack(hidden, w_query, w_key, w_value, w_out):
    column = 2 * w_key.shape[1]
    blocks = w_query.shape[1] // column + 1
    rows = w_query.shape[0] * blocks + w_out.shape[0]
    top = upper(w_query.shape[0]) * blocks + upper(w_out.shape[0])
    columns = like((hidden.shape[0], hidden.shape[1] // 2))
    return call(
        pack_kernel,
        (like((top, column)), like((rows - top, column)), columns, columns),
        [HB] * 5,
        scratch=[pltpu.SemaphoreType.DMA((12,))],
        name="pack",
    )(hidden, w_query, w_key, w_value, w_out)


def product(rows, top_ref, bottom_ref):
    depth = rows.shape[1]
    high, low = upper(depth), depth - upper(depth)
    parts = []
    for c in range(3):
        block = jnp.concatenate(
            [top_ref[c * high : (c + 1) * high], bottom_ref[c * low : (c + 1) * low]], axis=0
        )
        parts.append(jnp.dot(rows, block, preferred_element_type=jnp.float32))
    return jnp.concatenate(parts, axis=1)


def near_kernel(shards, place_ref, gain_ref, *refs):
    columns, weights = refs[:shards], refs[shards : 3 * shards - 2]
    partial_out, last_out, square_out, project_out, buf = refs[3 * shards - 2 :]
    mine, odd, plane = place_ref[0], place_ref[1], place_ref[2]
    square = 0.0
    for m in range(shards):
        rows = columns[m][...].astype(jnp.float32)
        square += jnp.sum(rows * rows, axis=-1, keepdims=True)
        gain = gain_ref[2 * (plane ^ m) + odd].astype(jnp.float32)
        buf[m] = (rows * gain).astype(jnp.bfloat16)
    square_out[...] = jnp.broadcast_to(square, square_out.shape)
    partial_out[...] = sum(
        product(buf[mine ^ j], weights[2 * j], weights[2 * j + 1]) for j in range(shards - 1)
    )
    last_out[...] = buf[mine ^ (shards - 1)]
    depth = project_out.shape[1]
    high = upper(depth)
    for j in range(shards - 1):
        project_out[j, :high] = weights[2 * j][weights[2 * j].shape[0] - high :]
        project_out[j, high:] = weights[2 * j + 1][weights[2 * j + 1].shape[0] - depth + high :]


def near_products(place, gain, columns, weights, depth):
    shards = len(columns)
    rows, width = columns[0].shape
    return call(
        functools.partial(near_kernel, shards),
        (
            like((rows, 3 * width), jnp.float32),
            like((rows, width)),
            like((rows, 128), jnp.float32),
            like((shards - 1, depth, weights[0].shape[1])),
        ),
        [SM, VM] + [VM] * (3 * shards - 2),
        scratch=[pltpu.VMEM((shards, rows, width), jnp.bfloat16)],
        busy=0.1,
        name="near_products",
    )(place, gain.reshape(2 * shards, 1, width), *columns, *weights)


def far_kernel(partial_ref, last_ref, square_ref, top_ref, bottom_ref, keep_out, send_out):
    total = partial_ref[...] + product(last_ref[...], top_ref, bottom_ref)
    tokens = keep_out.shape[0]
    width = total.shape[1]
    for out, first in ((keep_out, 0), (send_out, tokens)):
        out[:, :width] = total[first : first + tokens]
        out[:, width:] = square_ref[first : first + tokens, :]


def far_products(partial, last, square, top, bottom):
    rows, width = partial.shape
    out = like((rows // 2, width + 128), jnp.float32)
    return call(
        far_kernel,
        (out, out),
        [VM] * 5,
        busy=0.1,
        name="far_products",
    )(partial, last, square, top, bottom)


def rotate(rows, cosine, sine):
    lane = lax.broadcasted_iota(jnp.int32, (rows.shape[0], 128), 1)
    front = (lane % HD) < HD // 2
    slabs = []
    for s in range(rows.shape[1] // 128):
        slab = rows[:, s * 128 : (s + 1) * 128]
        other = jnp.where(
            front, -pltpu.roll(slab, 128 - HD // 2, 1), pltpu.roll(slab, HD // 2, 1)
        )
        slabs.append(slab * cosine + other * sine)
    return slabs


def place_queries(slabs, q_ref):
    rows = slabs[0].shape[0]
    factor = HD ** (-0.5) * math.log2(math.e)
    low = lax.broadcasted_iota(jnp.int32, (rows, 128), 1) < HD
    head = 0
    for s, slab in enumerate(slabs):
        slab = slab * factor
        rolled = pltpu.roll(slab, HD, 1)
        for odd_head in (0, 1):
            group = 0 if s < len(slabs) // 2 else 1
            keep = low if group == 0 else jnp.logical_not(low)
            value = jnp.where(keep, slab if group == odd_head else rolled, 0.0)
            q_ref[head * rows : (head + 1) * rows, :] = value.astype(jnp.bfloat16)
            head += 1


def one_over(x):
    near = pl.reciprocal(x, approx=True)
    return near * (2.0 - x * near)


def attend(q_ref, keys, values, mask):
    tokens = mask.shape[0]
    low = lax.broadcasted_iota(jnp.int32, values.shape, 1) < HD
    one = jnp.ones_like(values)
    mine = [jnp.where(low, values, one), jnp.where(low, one, values)]
    queries = q_ref.shape[0]
    mask = jnp.tile(mask, (QUERY_ROWS // tokens, 1))

    def score(start):
        return lax.dot_general(
            q_ref[start : start + QUERY_ROWS, :],
            keys,
            (((1,), (1,)), ((), ())),
            preferred_element_type=jnp.float32,
        )

    heads = []
    upcoming = score(0)
    for start in range(0, queries, QUERY_ROWS):
        scores = upcoming
        if start + QUERY_ROWS < queries:
            upcoming = score(start + QUERY_ROWS)
        scores = jnp.where(mask, scores, masked_score)
        peak = jnp.max(scores, axis=-1, keepdims=True)
        weights = jnp.exp2(scores - peak).astype(jnp.bfloat16)
        total = jnp.dot(
            weights, mine[start * 2 // queries], preferred_element_type=jnp.float32
        )
        mixed = total * one_over(pltpu.roll(total, HD, 1))
        heads += [mixed[i : i + tokens] for i in range(0, QUERY_ROWS, tokens)]
    return heads


def lay_out(heads, out_ref):
    low = lax.broadcasted_iota(jnp.int32, heads[0].shape, 1) < HD
    slabs = []
    for h, mixed in enumerate(heads):
        straight = (h % 2 == 0) == (h < len(heads) // 2)
        slabs.append(mixed if straight else pltpu.roll(mixed, HD, 1))
    for s in range(len(heads) // 2):
        both = jnp.where(low, slabs[2 * s], slabs[2 * s + 1])
        out_ref[:, s * 128 : (s + 1) * 128] = both.astype(jnp.bfloat16)


def attention_kernel(
    features,
    kv_width,
    length_ref,
    cos_ref,
    sin_ref,
    here_ref,
    there_ref,
    k_ref,
    v_ref,
    out_ref,
    nk_out,
    nv_out,
    nk_ref,
    nv_ref,
    q_ref,
    out_sems,
):
    length = length_ref[0]
    total = here_ref[...] + there_ref[...]
    width = total.shape[1] - 128
    scale = lax.rsqrt(total[:, width:] / features + norm_eps)
    total = total[:, :width] * jnp.tile(scale, (1, width // 128))
    tokens = total.shape[0]
    q_width = width - 2 * kv_width
    cosine, sine = cos_ref[...], sin_ref[...]
    (keys,) = rotate(total[:, q_width : q_width + kv_width], cosine, sine)
    nk_ref[...] = keys.astype(jnp.bfloat16)
    nv_ref[...] = total[:, q_width + kv_width :].astype(jnp.bfloat16)
    fresh = fetch([(nk_ref, nk_out), (nv_ref, nv_out)], out_sems)
    place_queries(rotate(total[:, :q_width], cosine, sine), q_ref)

    step = k_ref.shape[0] // CACHE_STEPS
    for cached in range(step, k_ref.shape[0] + 1, step):

        @pl.when((length > cached - step) & (length <= cached))
        def _(cached=cached):
            shape = (tokens, cached + tokens)
            column = lax.broadcasted_iota(jnp.int32, shape, 1)
            token = lax.broadcasted_iota(jnp.int32, shape, 0)
            limit = jnp.where(column < cached, length, cached + 1 + token)
            heads = attend(
                q_ref,
                jnp.concatenate([k_ref[:cached, :], nk_ref[...]], axis=0),
                jnp.concatenate([v_ref[:cached, :], nv_ref[...]], axis=0),
                column < limit,
            )
            lay_out(heads, out_ref)

    for copy in fresh:
        copy.wait()


def attention(length, features, cosine, sine, here, there, keys, values):
    tokens = here.shape[0]
    kv_width = keys.shape[1]
    q_width = here.shape[1] - 128 - 2 * kv_width
    queries = q_width // HD * tokens
    fresh = like((tokens, kv_width))
    return call(
        functools.partial(attention_kernel, features, kv_width),
        (like((tokens, q_width)), fresh, fresh),
        [SM, VM, VM, VM, VM, VM, VM],
        out_specs=(VM, HB, HB),
        scratch=[
            pltpu.VMEM(fresh.shape, jnp.bfloat16),
            pltpu.VMEM(fresh.shape, jnp.bfloat16),
            pltpu.VMEM((queries, 128), jnp.bfloat16),
            pltpu.SemaphoreType.DMA((2,)),
        ],
        busy=4.0,
        name="attention",
    )(length, cosine, sine, here, there, keys, values)


def out_kernel(distances, chips, place_ref, mixed_ref, own_ref, sibling_ref, *refs):
    last, outs = refs[:4], refs[4:]
    mine, odd = place_ref[0], place_ref[1]
    mixed = mixed_ref[...]
    width = outs[0].shape[1] // 2

    def store(out, weights):
        terms = [
            jnp.dot(mixed, w, preferred_element_type=jnp.float32).astype(jnp.bfloat16)
            for w in weights
        ]
        out[:, :width] = jnp.where(odd == 0, terms[0], terms[1])
        out[:, width:] = jnp.where(odd == 0, terms[1], terms[0])

    for out, m in zip(outs, distances, strict=True):
        j = mine ^ m

        @pl.when(j < chips - 1)
        def _(out=out, j=j):
            store(out, [own_ref[j], sibling_ref[j]])

        @pl.when(j == chips - 1)
        def _(out=out):
            halves = [h[h.shape[0] - last[2 + i % 2].shape[0] :] for i, h in enumerate(last)]
            store(out, [jnp.concatenate(halves[:2], axis=0), jnp.concatenate(halves[2:], axis=0)])


def project(distances, mixed, place, own, sibling, last):
    rows = mixed.shape[0]
    width = own.shape[2]
    return call(
        functools.partial(out_kernel, distances, own.shape[0] + 1),
        tuple(like((rows, 2 * width)) for _ in distances),
        [SM] + [VM] * 7,
        busy=1.0,
        name="project",
    )(place, mixed, own, sibling, *last)


def phases(length_now, row_count):
    positions = (length_now + jnp.arange(row_count, dtype=jnp.int32)).astype(jnp.float32)
    inverse = rope_base ** (-jnp.arange(0, HD, 2, dtype=jnp.int32).astype(jnp.float32) / HD)
    phase = positions[:, None] * jnp.tile(inverse, 4)[None, :]
    return jnp.cos(phase), jnp.sin(phase)


def swap(x, axis, mask):
    count = lax.axis_size(axis)
    return lax.ppermute(x, axis, [(i, i ^ mask) for i in range(count)])


CORE, SIDE_X, SIDE_Y = 1, 2, 4


def core(x):
    return swap(x, "req", CORE)


def per_device(
    hidden, norm_gain, w_query, w_key, w_value, w_out, cache_keys, cache_values, cache_lengths
):
    chip = lax.axis_index("req") // 2
    odd = lax.axis_index("req") % 2
    plane = lax.axis_index("tp")
    place = jnp.stack([chip ^ plane, odd, plane])
    length = lax.dynamic_slice_in_dim(cache_lengths, lax.axis_index("req"), 1, 0)
    tokens = hidden.shape[1]

    top, bottom, keep, send = pack(hidden[0], w_query, w_key, w_value, w_out)
    x_top, y_bottom = swap(top, "req", SIDE_X), swap(bottom, "req", SIDE_Y)
    got, top_later, bottom_later = lax.optimization_barrier((core(send), top, bottom))
    x_bottom, y_top = swap(bottom_later, "req", SIDE_X), swap(top_later, "req", SIDE_Y)
    columns = jnp.concatenate([keep, got], axis=0)
    two = swap(columns, "tp", 2)
    d_top, d_bottom = swap(x_top, "req", SIDE_Y), swap(y_bottom, "req", SIDE_X)
    _, _, columns_later, two_later = lax.optimization_barrier((x_top, y_bottom, columns, two))
    one = swap(columns_later, "tp", 1)
    _, two_later = lax.optimization_barrier((x_bottom, two_later))
    three = swap(two_later, "tp", 1)

    partial, last, square, o_near = near_products(
        place,
        norm_gain,
        [columns, one, two, three],
        [top, bottom, x_top, x_bottom, y_top, y_bottom],
        w_out.shape[0],
    )
    cosine, sine = phases(length[0], tokens)
    partial, cosine, sine = lax.optimization_barrier((partial, cosine, sine))
    here, there = far_products(partial, last, square, d_top, d_bottom)
    mixed, new_keys, new_values = attention(
        length,
        norm_gain.shape[0],
        cosine,
        sine,
        here,
        core(there),
        cache_keys[0],
        cache_values[0],
    )
    o_sibling = core(o_near)
    high = upper(w_out.shape[0])
    first, second = d_top.shape[0] - high, d_bottom.shape[0] - w_out.shape[0] + high
    o_last = [d_top, d_bottom, core(d_top[first:]), core(d_bottom[second:])]
    terms = {}
    terms[2], terms[3] = project((2, 3), mixed, place, o_near, o_sibling, o_last)
    mixed, terms[2], terms[3] = lax.optimization_barrier((mixed, terms[2], terms[3]))
    terms[0], terms[1] = project((0, 1), mixed, place, o_near, o_sibling, o_last)
    total = terms[0].astype(jnp.float32)
    for m in (1, 2, 3):
        total = total + swap(terms[m], "tp", m).astype(jnp.float32)
    return total.astype(jnp.bfloat16)[None], new_keys[None], new_values[None]


def general_rotate(tensor, cosine_table, sine_table):
    half_width = tensor.shape[-1] // 2
    front_half = tensor[..., :half_width]
    back_half = tensor[..., half_width:]
    return jnp.concatenate(
        [
            front_half * cosine_table - back_half * sine_table,
            back_half * cosine_table + front_half * sine_table,
        ],
        axis=-1,
    )


def general_phases(length_now, row_count):
    cosine, sine = phases(length_now, row_count)
    return cosine[:, None, : HD // 2], sine[:, None, : HD // 2]


def group_queries(flat_queries, key_heads, group_size, head_width):
    token_count = flat_queries.shape[0]
    shaped = flat_queries.reshape(token_count, key_heads, group_size, head_width).transpose(
        1, 2, 0, 3
    )
    return shaped.reshape(key_heads, group_size * token_count, head_width)


def attend_block(running, grouped, key_block, value_block, visible):
    peak_old, total_old, accum_old = running
    scores = jnp.einsum(
        "gqd,kgd->gqk", grouped, key_block, preferred_element_type=jnp.float32
    ) * grouped.shape[-1] ** (-0.5)
    scores = jnp.where(visible, scores, masked_score)
    peak_new = jnp.maximum(peak_old, jnp.max(scores, axis=-1))
    weights = jnp.where(visible, jnp.exp(scores - peak_new[..., None]), 0.0)
    factor = jnp.exp(peak_old - peak_new)
    total_new = total_old * factor + jnp.sum(weights, axis=-1)
    accum_new = accum_old * factor[:, None, :] + jnp.einsum(
        "gqk,kgd->gdq",
        weights.astype(jnp.bfloat16),
        value_block,
        preferred_element_type=jnp.float32,
    )
    return (peak_new, total_new, accum_new)


def cache_pass(
    running, grouped, key_cache, value_cache, buffer_first, lower_row, upper_row, block_rows
):
    first_block = lower_row // block_rows
    last_block = jnp.where(
        lower_row < upper_row, (upper_row + block_rows - 1) // block_rows, first_block
    )

    def step_body(block_index, running_now):
        position_first = block_index * block_rows
        local_first = position_first - buffer_first
        key_block = lax.dynamic_slice_in_dim(key_cache, local_first, block_rows, 0)
        value_block = lax.dynamic_slice_in_dim(value_cache, local_first, block_rows, 0)
        positions = position_first + jnp.arange(block_rows, dtype=jnp.int32)
        visible = ((positions >= lower_row) & (positions < upper_row))[None, None, :]
        return attend_block(running_now, grouped, key_block, value_block, visible)

    return lax.fori_loop(first_block, last_block, step_body, running)


def new_pass(running, grouped, fresh_keys, fresh_values, token_count, block_rows):
    token_of_row = jnp.arange(grouped.shape[1], dtype=jnp.int32) % token_count
    positions = 0 + jnp.arange(block_rows, dtype=jnp.int32)
    visible = (positions[None, :] <= token_of_row[:, None])[None]
    running = attend_block(running, grouped, fresh_keys, fresh_values, visible)
    return running


def general_device(
    hidden, norm_gain, w_query, w_key, w_value, w_out, cache_keys, cache_values, cache_lengths
):
    token_count = hidden.shape[1]
    gathered = lax.all_gather(hidden[0], "tp", axis=1, tiled=True)
    as_float = gathered.astype(jnp.float32)
    mean_square = jnp.mean(as_float * as_float, axis=-1, keepdims=True)
    normed = (as_float * lax.rsqrt(mean_square + norm_eps) * norm_gain.astype(jnp.float32)).astype(
        jnp.bfloat16
    )
    query_width = w_query.shape[1]
    key_width = w_key.shape[1]
    query_sum = jnp.dot(
        normed,
        lax.all_gather(w_query, "req", axis=0, tiled=True),
        preferred_element_type=jnp.float32,
    )
    key_sum = jnp.dot(
        normed, lax.all_gather(w_key, "req", axis=0, tiled=True), preferred_element_type=jnp.float32
    )
    value_sum = jnp.dot(
        normed,
        lax.all_gather(w_value, "req", axis=0, tiled=True),
        preferred_element_type=jnp.float32,
    )
    device_index = lax.axis_index("req")
    length_own = cache_lengths[device_index]
    head_width = HD
    local_heads = query_width // head_width
    key_heads = key_width // head_width
    group_size = local_heads // key_heads
    cosine_table, sine_table = general_phases(length_own, token_count)
    flat_queries = (
        general_rotate(query_sum.reshape(token_count, local_heads, head_width), cosine_table, sine_table)
        .astype(jnp.bfloat16)
        .reshape(token_count, query_width)
    )
    fresh_keys = general_rotate(
        key_sum.reshape(token_count, key_heads, head_width), cosine_table, sine_table
    ).astype(jnp.bfloat16)
    fresh_values = value_sum.reshape(token_count, key_heads, head_width).astype(jnp.bfloat16)
    grouped = group_queries(flat_queries, key_heads, group_size, head_width)
    cache_rows = cache_keys.shape[1]
    key_cache = cache_keys[0].reshape(cache_rows, key_heads, head_width)
    value_cache = cache_values[0].reshape(cache_rows, key_heads, head_width)
    block_cache = min(512, cache_rows // 2)
    block_new = min(512, token_count)
    query_count = group_size * token_count
    start_state = (
        jnp.full((key_heads, query_count), masked_score, jnp.float32),
        jnp.zeros((key_heads, query_count), jnp.float32),
        jnp.zeros((key_heads, head_width, query_count), jnp.float32),
    )
    own_part = cache_pass(
        start_state, grouped, key_cache, value_cache, 0, 0, length_own, block_cache
    )
    combined = new_pass(own_part, grouped, fresh_keys, fresh_values, token_count, block_new)
    accumulated = combined[2] / combined[1][:, None, :]
    mixed_heads = (
        accumulated.reshape(key_heads, head_width, group_size, token_count)
        .transpose(3, 0, 2, 1)
        .reshape(token_count, query_width)
        .astype(jnp.bfloat16)
    )
    partial_out = jnp.dot(
        mixed_heads,
        lax.all_gather(w_out, "req", axis=1, tiled=True),
        preferred_element_type=jnp.float32,
    )
    summed = lax.psum_scatter(
        partial_out.astype(jnp.bfloat16), "tp", scatter_dimension=1, tiled=True
    )
    return (
        summed[None],
        fresh_keys.reshape(token_count, key_width)[None],
        fresh_values.reshape(token_count, key_width)[None],
    )


def solution(mesh):
    in_specs = (
        P("req", None, "tp"),
        P(),
        P("req", "tp"),
        P("req", "tp"),
        P("req", "tp"),
        P("tp", "req"),
        P("req", None, "tp"),
        P("req", None, "tp"),
        P(),
    )
    out_specs = (P("req", None, "tp"), P("req", None, "tp"), P("req", None, "tp"))
    ringed = mesh.shape["req"] == 8 and mesh.shape["tp"] == 4
    return jax.shard_map(
        per_device if ringed else general_device,
        mesh=mesh,
        in_specs=in_specs,
        out_specs=out_specs,
        check_vma=False,
    )
```

```python
import functools
import math

import jax
import jax.numpy as jnp
from jax import lax
from jax.experimental import pallas as pl
from jax.experimental.pallas import tpu as pltpu
from jax.sharding import PartitionSpec as P

HD = 64
rope_base = 1000000.0
norm_eps = 1e-05
masked_score = -1e30
CACHE_STEPS = 4
QUERY_ROWS = 256
SIXTEENTHS = 8
FLOPS_PER_US = 1.1e9
VMEM_BYTES = 24 * 1024 * 1024

VM = pl.BlockSpec(memory_space=pltpu.VMEM)
HB = pl.BlockSpec(memory_space=pltpu.HBM)
SM = pl.BlockSpec(memory_space=pltpu.SMEM)


def call(kernel, out_shape, in_specs, scratch=(), busy=1.0, name=None, out_specs=None):
    run = pl.pallas_call(
        kernel,
        out_shape=out_shape,
        in_specs=in_specs,
        out_specs=out_specs or jax.tree.map(lambda _: VM, out_shape),
        scratch_shapes=list(scratch),
        compiler_params=pltpu.CompilerParams(vmem_limit_bytes=VMEM_BYTES),
        cost_estimate=pl.CostEstimate(
            flops=int(busy * FLOPS_PER_US), bytes_accessed=1 << 16, transcendentals=0
        ),
        name=name,
    )

    def placed(*operands):
        return run(
            *[
                pltpu.with_memory_space_constraint(x, pltpu.HBM) if spec is HB else x
                for x, spec in zip(operands, in_specs, strict=True)
            ]
        )

    return placed


def like(shape, dtype=jnp.bfloat16):
    return jax.ShapeDtypeStruct(shape, dtype)


def fetch(pairs, sems):
    copies = [pltpu.make_async_copy(src, dst, sems.at[i]) for i, (src, dst) in enumerate(pairs)]
    for copy in copies:
        copy.start()
    return copies


def upper(rows):
    return rows * SIXTEENTHS // 16


def pack_kernel(
    hidden_ref,
    wq_ref,
    wk_ref,
    wv_ref,
    wo_ref,
    top_out,
    bottom_out,
    keep_out,
    send_out,
    sems,
):
    odd = lax.axis_index("req") % 2
    rows, width = wq_ref.shape
    column, kv = top_out.shape[1], wk_ref.shape[1]
    pairs = []
    for part, out in enumerate((top_out, bottom_out)):
        start, size = part * upper(rows), (upper(rows), rows - upper(rows))[part]
        source = pl.ds(start, size)
        first = 0
        for c in range(width // column):
            pairs.append((wq_ref.at[source, pl.ds(c * column, column)], out.at[pl.ds(first, size)]))
            first += size
        for i, w in enumerate((wk_ref, wv_ref)):
            pairs.append((w.at[source], out.at[pl.ds(first, size), pl.ds(i * kv, kv)]))
        first += size
        depth = wo_ref.shape[0]
        start, size = part * upper(depth), (upper(depth), depth - upper(depth))[part]
        pairs.append((wo_ref.at[pl.ds(start, size)], out.at[pl.ds(first, size)]))
    half = keep_out.shape[1]
    mine = pl.ds(pl.multiple_of(odd * half, half), half)
    other = pl.ds(pl.multiple_of((1 - odd) * half, half), half)
    pairs += [(hidden_ref.at[:, other], send_out), (hidden_ref.at[:, mine], keep_out)]
    for copy in fetch(pairs, sems):
        copy.wait()


def pack(hidden, w_query, w_key, w_value, w_out):
    column = 2 * w_key.shape[1]
    blocks = w_query.shape[1] // column + 1
    rows = w_query.shape[0] * blocks + w_out.shape[0]
    top = upper(w_query.shape[0]) * blocks + upper(w_out.shape[0])
    columns = like((hidden.shape[0], hidden.shape[1] // 2))
    return call(
        pack_kernel,
        (like((top, column)), like((rows - top, column)), columns, columns),
        [HB] * 5,
        scratch=[pltpu.SemaphoreType.DMA((12,))],
        name="pack",
    )(hidden, w_query, w_key, w_value, w_out)


def product(rows, top_ref, bottom_ref):
    depth = rows.shape[1]
    high, low = upper(depth), depth - upper(depth)
    parts = []
    for c in range(3):
        block = jnp.concatenate(
            [top_ref[c * high : (c + 1) * high], bottom_ref[c * low : (c + 1) * low]], axis=0
        )
        parts.append(jnp.dot(rows, block, preferred_element_type=jnp.float32))
    return jnp.concatenate(parts, axis=1)


def near_kernel(shards, place_ref, gain_ref, *refs):
    columns, weights = refs[:shards], refs[shards : 3 * shards - 2]
    partial_out, last_out, square_out, project_out, buf = refs[3 * shards - 2 :]
    mine, odd, plane = place_ref[0], place_ref[1], place_ref[2]
    square = 0.0
    for m in range(shards):
        rows = columns[m][...].astype(jnp.float32)
        square += jnp.sum(rows * rows, axis=-1, keepdims=True)
        gain = gain_ref[2 * (plane ^ m) + odd].astype(jnp.float32)
        buf[m] = (rows * gain).astype(jnp.bfloat16)
    square_out[...] = jnp.broadcast_to(square, square_out.shape)
    partial_out[...] = sum(
        product(buf[mine ^ j], weights[2 * j], weights[2 * j + 1]) for j in range(shards - 1)
    )
    last_out[...] = buf[mine ^ (shards - 1)]
    depth = project_out.shape[1]
    high = upper(depth)
    for j in range(shards - 1):
        project_out[j, :high] = weights[2 * j][weights[2 * j].shape[0] - high :]
        project_out[j, high:] = weights[2 * j + 1][weights[2 * j + 1].shape[0] - depth + high :]


def near_products(place, gain, columns, weights, depth):
    shards = len(columns)
    rows, width = columns[0].shape
    return call(
        functools.partial(near_kernel, shards),
        (
            like((rows, 3 * width), jnp.float32),
            like((rows, width)),
            like((rows, 128), jnp.float32),
            like((shards - 1, depth, weights[0].shape[1])),
        ),
        [SM, VM] + [VM] * (3 * shards - 2),
        scratch=[pltpu.VMEM((shards, rows, width), jnp.bfloat16)],
        busy=0.1,
        name="near_products",
    )(place, gain.reshape(2 * shards, 1, width), *columns, *weights)


def far_kernel(partial_ref, last_ref, square_ref, top_ref, bottom_ref, keep_out, send_out):
    total = partial_ref[...] + product(last_ref[...], top_ref, bottom_ref)
    tokens = keep_out.shape[0]
    width = total.shape[1]
    for out, first in ((keep_out, 0), (send_out, tokens)):
        out[:, :width] = total[first : first + tokens]
        out[:, width:] = square_ref[first : first + tokens, :]


def far_products(partial, last, square, top, bottom):
    rows, width = partial.shape
    out = like((rows // 2, width + 128), jnp.float32)
    return call(
        far_kernel,
        (out, out),
        [VM] * 5,
        busy=0.1,
        name="far_products",
    )(partial, last, square, top, bottom)


def rotate(rows, cosine, sine):
    lane = lax.broadcasted_iota(jnp.int32, (rows.shape[0], 128), 1)
    front = (lane % HD) < HD // 2
    slabs = []
    for s in range(rows.shape[1] // 128):
        slab = rows[:, s * 128 : (s + 1) * 128]
        other = jnp.where(
            front, -pltpu.roll(slab, 128 - HD // 2, 1), pltpu.roll(slab, HD // 2, 1)
        )
        slabs.append(slab * cosine + other * sine)
    return slabs


def place_queries(slabs, q_ref):
    rows = slabs[0].shape[0]
    factor = HD ** (-0.5) * math.log2(math.e)
    low = lax.broadcasted_iota(jnp.int32, (rows, 128), 1) < HD
    head = 0
    for s, slab in enumerate(slabs):
        slab = slab * factor
        rolled = pltpu.roll(slab, HD, 1)
        for odd_head in (0, 1):
            group = 0 if s < len(slabs) // 2 else 1
            keep = low if group == 0 else jnp.logical_not(low)
            value = jnp.where(keep, slab if group == odd_head else rolled, 0.0)
            q_ref[head * rows : (head + 1) * rows, :] = value.astype(jnp.bfloat16)
            head += 1


def one_over(x):
    near = pl.reciprocal(x, approx=True)
    return near * (2.0 - x * near)


def attend(q_ref, keys, values, mask):
    tokens = mask.shape[0]
    low = lax.broadcasted_iota(jnp.int32, values.shape, 1) < HD
    one = jnp.ones_like(values)
    mine = [jnp.where(low, values, one), jnp.where(low, one, values)]
    queries = q_ref.shape[0]
    mask = jnp.tile(mask, (QUERY_ROWS // tokens, 1))

    def score(start):
        return lax.dot_general(
            q_ref[start : start + QUERY_ROWS, :],
            keys,
            (((1,), (1,)), ((), ())),
            preferred_element_type=jnp.float32,
        )

    heads = []
    upcoming = score(0)
    for start in range(0, queries, QUERY_ROWS):
        scores = upcoming
        if start + QUERY_ROWS < queries:
            upcoming = score(start + QUERY_ROWS)
        sure = scores.shape[1] - mask.shape[1]
        unsure = jnp.where(mask, scores[:, sure:], masked_score)
        scores = jnp.concatenate([scores[:, :sure], unsure], axis=1) if sure else unsure
        peak = jnp.max(scores, axis=-1, keepdims=True)
        weights = jnp.exp2(scores - peak).astype(jnp.bfloat16)
        total = jnp.dot(
            weights, mine[start * 2 // queries], preferred_element_type=jnp.float32
        )
        mixed = total * one_over(pltpu.roll(total, HD, 1))
        heads += [mixed[i : i + tokens] for i in range(0, QUERY_ROWS, tokens)]
    return heads


def lay_out(heads, out_ref):
    low = lax.broadcasted_iota(jnp.int32, heads[0].shape, 1) < HD
    slabs = []
    for h, mixed in enumerate(heads):
        straight = (h % 2 == 0) == (h < len(heads) // 2)
        slabs.append(mixed if straight else pltpu.roll(mixed, HD, 1))
    for s in range(len(heads) // 2):
        both = jnp.where(low, slabs[2 * s], slabs[2 * s + 1])
        out_ref[:, s * 128 : (s + 1) * 128] = both.astype(jnp.bfloat16)


def attention_kernel(
    features,
    kv_width,
    length_ref,
    cos_ref,
    sin_ref,
    here_ref,
    there_ref,
    k_ref,
    v_ref,
    out_ref,
    nk_out,
    nv_out,
    nk_ref,
    nv_ref,
    q_ref,
    out_sems,
):
    length = length_ref[0]
    total = here_ref[...] + there_ref[...]
    width = total.shape[1] - 128
    scale = lax.rsqrt(total[:, width:] / features + norm_eps)
    total = total[:, :width] * jnp.tile(scale, (1, width // 128))
    tokens = total.shape[0]
    q_width = width - 2 * kv_width
    cosine, sine = cos_ref[...], sin_ref[...]
    (keys,) = rotate(total[:, q_width : q_width + kv_width], cosine, sine)
    nk_ref[...] = keys.astype(jnp.bfloat16)
    nv_ref[...] = total[:, q_width + kv_width :].astype(jnp.bfloat16)
    fresh = fetch([(nk_ref, nk_out), (nv_ref, nv_out)], out_sems)
    place_queries(rotate(total[:, :q_width], cosine, sine), q_ref)

    step = k_ref.shape[0] // CACHE_STEPS
    for cached in range(step, k_ref.shape[0] + 1, step):

        @pl.when((length > cached - step) & (length <= cached))
        def _(cached=cached):
            shape = (tokens, step + tokens)
            column = cached - step + lax.broadcasted_iota(jnp.int32, shape, 1)
            token = lax.broadcasted_iota(jnp.int32, shape, 0)
            limit = jnp.where(column < cached, length, cached + 1 + token)
            heads = attend(
                q_ref,
                jnp.concatenate([k_ref[:cached, :], nk_ref[...]], axis=0),
                jnp.concatenate([v_ref[:cached, :], nv_ref[...]], axis=0),
                column < limit,
            )
            lay_out(heads, out_ref)

    for copy in fresh:
        copy.wait()


def attention(length, features, cosine, sine, here, there, keys, values):
    tokens = here.shape[0]
    kv_width = keys.shape[1]
    q_width = here.shape[1] - 128 - 2 * kv_width
    queries = q_width // HD * tokens
    fresh = like((tokens, kv_width))
    return call(
        functools.partial(attention_kernel, features, kv_width),
        (like((tokens, q_width)), fresh, fresh),
        [SM, VM, VM, VM, VM, VM, VM],
        out_specs=(VM, HB, HB),
        scratch=[
            pltpu.VMEM(fresh.shape, jnp.bfloat16),
            pltpu.VMEM(fresh.shape, jnp.bfloat16),
            pltpu.VMEM((queries, 128), jnp.bfloat16),
            pltpu.SemaphoreType.DMA((2,)),
        ],
        busy=4.0,
        name="attention",
    )(length, cosine, sine, here, there, keys, values)


def out_kernel(distances, chips, place_ref, mixed_ref, own_ref, sibling_ref, *refs):
    last, outs = refs[:4], refs[4:]
    mine, odd = place_ref[0], place_ref[1]
    mixed = mixed_ref[...]
    width = outs[0].shape[1] // 2

    def store(out, weights):
        terms = [
            jnp.dot(mixed, w, preferred_element_type=jnp.float32).astype(jnp.bfloat16)
            for w in weights
        ]
        out[:, :width] = jnp.where(odd == 0, terms[0], terms[1])
        out[:, width:] = jnp.where(odd == 0, terms[1], terms[0])

    for out, m in zip(outs, distances, strict=True):
        j = mine ^ m

        @pl.when(j < chips - 1)
        def _(out=out, j=j):
            store(out, [own_ref[j], sibling_ref[j]])

        @pl.when(j == chips - 1)
        def _(out=out):
            halves = [h[h.shape[0] - last[2 + i % 2].shape[0] :] for i, h in enumerate(last)]
            store(out, [jnp.concatenate(halves[:2], axis=0), jnp.concatenate(halves[2:], axis=0)])


def project(distances, mixed, place, own, sibling, last):
    rows = mixed.shape[0]
    width = own.shape[2]
    return call(
        functools.partial(out_kernel, distances, own.shape[0] + 1),
        tuple(like((rows, 2 * width)) for _ in distances),
        [SM] + [VM] * 7,
        busy=1.0,
        name="project",
    )(place, mixed, own, sibling, *last)


def phases(length_now, row_count):
    positions = (length_now + jnp.arange(row_count, dtype=jnp.int32)).astype(jnp.float32)
    inverse = rope_base ** (-jnp.arange(0, HD, 2, dtype=jnp.int32).astype(jnp.float32) / HD)
    phase = positions[:, None] * jnp.tile(inverse, 4)[None, :]
    return jnp.cos(phase), jnp.sin(phase)


def swap(x, axis, mask):
    count = lax.axis_size(axis)
    return lax.ppermute(x, axis, [(i, i ^ mask) for i in range(count)])


CORE, SIDE_X, SIDE_Y = 1, 2, 4


def core(x):
    return swap(x, "req", CORE)


def per_device(
    hidden, norm_gain, w_query, w_key, w_value, w_out, cache_keys, cache_values, cache_lengths
):
    chip = lax.axis_index("req") // 2
    odd = lax.axis_index("req") % 2
    plane = lax.axis_index("tp")
    place = jnp.stack([chip ^ plane, odd, plane])
    length = lax.dynamic_slice_in_dim(cache_lengths, lax.axis_index("req"), 1, 0)
    tokens = hidden.shape[1]

    top, bottom, keep, send = pack(hidden[0], w_query, w_key, w_value, w_out)
    x_top, y_bottom = swap(top, "req", SIDE_X), swap(bottom, "req", SIDE_Y)
    got, top_later, bottom_later = lax.optimization_barrier((core(send), top, bottom))
    x_bottom, y_top = swap(bottom_later, "req", SIDE_X), swap(top_later, "req", SIDE_Y)
    columns = jnp.concatenate([keep, got], axis=0)
    two = swap(columns, "tp", 2)
    d_top, d_bottom = swap(x_top, "req", SIDE_Y), swap(y_bottom, "req", SIDE_X)
    _, _, columns_later, two_later = lax.optimization_barrier((x_top, y_bottom, columns, two))
    one = swap(columns_later, "tp", 1)
    _, two_later = lax.optimization_barrier((x_bottom, two_later))
    three = swap(two_later, "tp", 1)

    partial, last, square, o_near = near_products(
        place,
        norm_gain,
        [columns, one, two, three],
        [top, bottom, x_top, x_bottom, y_top, y_bottom],
        w_out.shape[0],
    )
    cosine, sine = phases(length[0], tokens)
    partial, cosine, sine = lax.optimization_barrier((partial, cosine, sine))
    here, there = far_products(partial, last, square, d_top, d_bottom)
    there, o_near = lax.optimization_barrier((there, o_near))
    mixed, new_keys, new_values = attention(
        length,
        norm_gain.shape[0],
        cosine,
        sine,
        here,
        core(there),
        cache_keys[0],
        cache_values[0],
    )
    o_sibling = core(o_near)
    high = upper(w_out.shape[0])
    first, second = d_top.shape[0] - high, d_bottom.shape[0] - w_out.shape[0] + high
    o_last = [d_top, d_bottom, core(d_top[first:]), core(d_bottom[second:])]
    terms = {}
    terms[2], terms[3] = project((2, 3,), mixed, place, o_near, o_sibling, o_last)
    mixed, terms[2], terms[3] = lax.optimization_barrier((mixed, terms[2], terms[3]))
    terms[0], terms[1] = project((0, 1,), mixed, place, o_near, o_sibling, o_last)
    total = terms[0].astype(jnp.float32)
    for m in (3, 1, 2):
        total = total + swap(terms[m], "tp", m).astype(jnp.float32)
    return total.astype(jnp.bfloat16)[None], new_keys[None], new_values[None]


def general_rotate(tensor, cosine_table, sine_table):
    half_width = tensor.shape[-1] // 2
    front_half = tensor[..., :half_width]
    back_half = tensor[..., half_width:]
    return jnp.concatenate(
        [
            front_half * cosine_table - back_half * sine_table,
            back_half * cosine_table + front_half * sine_table,
        ],
        axis=-1,
    )


def general_phases(length_now, row_count):
    cosine, sine = phases(length_now, row_count)
    return cosine[:, None, : HD // 2], sine[:, None, : HD // 2]


def group_queries(flat_queries, key_heads, group_size, head_width):
    token_count = flat_queries.shape[0]
    shaped = flat_queries.reshape(token_count, key_heads, group_size, head_width).transpose(
        1, 2, 0, 3
    )
    return shaped.reshape(key_heads, group_size * token_count, head_width)


def attend_block(running, grouped, key_block, value_block, visible):
    peak_old, total_old, accum_old = running
    scores = jnp.einsum(
        "gqd,kgd->gqk", grouped, key_block, preferred_element_type=jnp.float32
    ) * grouped.shape[-1] ** (-0.5)
    scores = jnp.where(visible, scores, masked_score)
    peak_new = jnp.maximum(peak_old, jnp.max(scores, axis=-1))
    weights = jnp.where(visible, jnp.exp(scores - peak_new[..., None]), 0.0)
    factor = jnp.exp(peak_old - peak_new)
    total_new = total_old * factor + jnp.sum(weights, axis=-1)
    accum_new = accum_old * factor[:, None, :] + jnp.einsum(
        "gqk,kgd->gdq",
        weights.astype(jnp.bfloat16),
        value_block,
        preferred_element_type=jnp.float32,
    )
    return (peak_new, total_new, accum_new)


def cache_pass(
    running, grouped, key_cache, value_cache, buffer_first, lower_row, upper_row, block_rows
):
    first_block = lower_row // block_rows
    last_block = jnp.where(
        lower_row < upper_row, (upper_row + block_rows - 1) // block_rows, first_block
    )

    def step_body(block_index, running_now):
        position_first = block_index * block_rows
        local_first = position_first - buffer_first
        key_block = lax.dynamic_slice_in_dim(key_cache, local_first, block_rows, 0)
        value_block = lax.dynamic_slice_in_dim(value_cache, local_first, block_rows, 0)
        positions = position_first + jnp.arange(block_rows, dtype=jnp.int32)
        visible = ((positions >= lower_row) & (positions < upper_row))[None, None, :]
        return attend_block(running_now, grouped, key_block, value_block, visible)

    return lax.fori_loop(first_block, last_block, step_body, running)


def new_pass(running, grouped, fresh_keys, fresh_values, token_count, block_rows):
    token_of_row = jnp.arange(grouped.shape[1], dtype=jnp.int32) % token_count
    positions = 0 + jnp.arange(block_rows, dtype=jnp.int32)
    visible = (positions[None, :] <= token_of_row[:, None])[None]
    running = attend_block(running, grouped, fresh_keys, fresh_values, visible)
    return running


def general_device(
    hidden, norm_gain, w_query, w_key, w_value, w_out, cache_keys, cache_values, cache_lengths
):
    token_count = hidden.shape[1]
    gathered = lax.all_gather(hidden[0], "tp", axis=1, tiled=True)
    as_float = gathered.astype(jnp.float32)
    mean_square = jnp.mean(as_float * as_float, axis=-1, keepdims=True)
    normed = (as_float * lax.rsqrt(mean_square + norm_eps) * norm_gain.astype(jnp.float32)).astype(
        jnp.bfloat16
    )
    query_width = w_query.shape[1]
    key_width = w_key.shape[1]
    query_sum = jnp.dot(
        normed,
        lax.all_gather(w_query, "req", axis=0, tiled=True),
        preferred_element_type=jnp.float32,
    )
    key_sum = jnp.dot(
        normed, lax.all_gather(w_key, "req", axis=0, tiled=True), preferred_element_type=jnp.float32
    )
    value_sum = jnp.dot(
        normed,
        lax.all_gather(w_value, "req", axis=0, tiled=True),
        preferred_element_type=jnp.float32,
    )
    device_index = lax.axis_index("req")
    length_own = cache_lengths[device_index]
    head_width = HD
    local_heads = query_width // head_width
    key_heads = key_width // head_width
    group_size = local_heads // key_heads
    cosine_table, sine_table = general_phases(length_own, token_count)
    flat_queries = (
        general_rotate(query_sum.reshape(token_count, local_heads, head_width), cosine_table, sine_table)
        .astype(jnp.bfloat16)
        .reshape(token_count, query_width)
    )
    fresh_keys = general_rotate(
        key_sum.reshape(token_count, key_heads, head_width), cosine_table, sine_table
    ).astype(jnp.bfloat16)
    fresh_values = value_sum.reshape(token_count, key_heads, head_width).astype(jnp.bfloat16)
    grouped = group_queries(flat_queries, key_heads, group_size, head_width)
    cache_rows = cache_keys.shape[1]
    key_cache = cache_keys[0].reshape(cache_rows, key_heads, head_width)
    value_cache = cache_values[0].reshape(cache_rows, key_heads, head_width)
    block_cache = min(512, cache_rows // 2)
    block_new = min(512, token_count)
    query_count = group_size * token_count
    start_state = (
        jnp.full((key_heads, query_count), masked_score, jnp.float32),
        jnp.zeros((key_heads, query_count), jnp.float32),
        jnp.zeros((key_heads, head_width, query_count), jnp.float32),
    )
    own_part = cache_pass(
        start_state, grouped, key_cache, value_cache, 0, 0, length_own, block_cache
    )
    combined = new_pass(own_part, grouped, fresh_keys, fresh_values, token_count, block_new)
    accumulated = combined[2] / combined[1][:, None, :]
    mixed_heads = (
        accumulated.reshape(key_heads, head_width, group_size, token_count)
        .transpose(3, 0, 2, 1)
        .reshape(token_count, query_width)
        .astype(jnp.bfloat16)
    )
    partial_out = jnp.dot(
        mixed_heads,
        lax.all_gather(w_out, "req", axis=1, tiled=True),
        preferred_element_type=jnp.float32,
    )
    summed = lax.psum_scatter(
        partial_out.astype(jnp.bfloat16), "tp", scatter_dimension=1, tiled=True
    )
    return (
        summed[None],
        fresh_keys.reshape(token_count, key_width)[None],
        fresh_values.reshape(token_count, key_width)[None],
    )


def solution(mesh):
    in_specs = (
        P("req", None, "tp"),
        P(),
        P("req", "tp"),
        P("req", "tp"),
        P("req", "tp"),
        P("tp", "req"),
        P("req", None, "tp"),
        P("req", None, "tp"),
        P(),
    )
    out_specs = (P("req", None, "tp"), P("req", None, "tp"), P("req", None, "tp"))
    ringed = mesh.shape["req"] == 8 and mesh.shape["tp"] == 4
    return jax.shard_map(
        per_device if ringed else general_device,
        mesh=mesh,
        in_specs=in_specs,
        out_specs=out_specs,
        check_vma=False,
    )
```

```python
import functools
import math

import jax
import jax.numpy as jnp
from jax import lax
from jax.experimental import pallas as pl
from jax.experimental.pallas import tpu as pltpu
from jax.sharding import PartitionSpec as P

HD = 64
rope_base = 1000000.0
norm_eps = 1e-05
masked_score = -1e30
CACHE_STEPS = 8
QUERY_ROWS = 512
SIXTEENTHS = 8
FLOPS_PER_US = 1.1e9
VMEM_BYTES = 24 * 1024 * 1024

VM = pl.BlockSpec(memory_space=pltpu.VMEM)
HB = pl.BlockSpec(memory_space=pltpu.HBM)
SM = pl.BlockSpec(memory_space=pltpu.SMEM)


def call(kernel, out_shape, in_specs, scratch=(), busy=1.0, name=None, out_specs=None):
    run = pl.pallas_call(
        kernel,
        out_shape=out_shape,
        in_specs=in_specs,
        out_specs=out_specs or jax.tree.map(lambda _: VM, out_shape),
        scratch_shapes=list(scratch),
        compiler_params=pltpu.CompilerParams(vmem_limit_bytes=VMEM_BYTES),
        cost_estimate=pl.CostEstimate(
            flops=int(busy * FLOPS_PER_US), bytes_accessed=1 << 16, transcendentals=0
        ),
        name=name,
    )

    def placed(*operands):
        return run(
            *[
                pltpu.with_memory_space_constraint(x, pltpu.HBM) if spec is HB else x
                for x, spec in zip(operands, in_specs, strict=True)
            ]
        )

    return placed


def like(shape, dtype=jnp.bfloat16):
    return jax.ShapeDtypeStruct(shape, dtype)


def fetch(pairs, sems):
    copies = [pltpu.make_async_copy(src, dst, sems.at[i]) for i, (src, dst) in enumerate(pairs)]
    for copy in copies:
        copy.start()
    return copies


def upper(rows):
    return rows * SIXTEENTHS // 16


def pack_kernel(
    hidden_ref,
    wq_ref,
    wk_ref,
    wv_ref,
    wo_ref,
    top_out,
    bottom_out,
    keep_out,
    send_out,
    sems,
):
    odd = lax.axis_index("req") % 2
    rows, width = wq_ref.shape
    column, kv = top_out.shape[1], wk_ref.shape[1]
    pairs = []
    for part, out in enumerate((top_out, bottom_out)):
        start, size = part * upper(rows), (upper(rows), rows - upper(rows))[part]
        source = pl.ds(start, size)
        first = 0
        for c in range(width // column):
            pairs.append((wq_ref.at[source, pl.ds(c * column, column)], out.at[pl.ds(first, size)]))
            first += size
        for i, w in enumerate((wk_ref, wv_ref)):
            pairs.append((w.at[source], out.at[pl.ds(first, size), pl.ds(i * kv, kv)]))
        first += size
        depth = wo_ref.shape[0]
        start, size = part * upper(depth), (upper(depth), depth - upper(depth))[part]
        pairs.append((wo_ref.at[pl.ds(start, size)], out.at[pl.ds(first, size)]))
    half = keep_out.shape[1]
    mine = pl.ds(pl.multiple_of(odd * half, half), half)
    other = pl.ds(pl.multiple_of((1 - odd) * half, half), half)
    pairs += [(hidden_ref.at[:, other], send_out), (hidden_ref.at[:, mine], keep_out)]
    for copy in fetch(pairs, sems):
        copy.wait()


def pack(hidden, w_query, w_key, w_value, w_out):
    column = 2 * w_key.shape[1]
    blocks = w_query.shape[1] // column + 1
    rows = w_query.shape[0] * blocks + w_out.shape[0]
    top = upper(w_query.shape[0]) * blocks + upper(w_out.shape[0])
    columns = like((hidden.shape[0], hidden.shape[1] // 2))
    return call(
        pack_kernel,
        (like((top, column)), like((rows - top, column)), columns, columns),
        [HB] * 5,
        scratch=[pltpu.SemaphoreType.DMA((12,))],
        name="pack",
    )(hidden, w_query, w_key, w_value, w_out)


def product(rows, top_ref, bottom_ref):
    depth = rows.shape[1]
    high, low = upper(depth), depth - upper(depth)
    parts = []
    for c in range(3):
        block = jnp.concatenate(
            [top_ref[c * high : (c + 1) * high], bottom_ref[c * low : (c + 1) * low]], axis=0
        )
        parts.append(jnp.dot(rows, block, preferred_element_type=jnp.float32))
    return jnp.concatenate(parts, axis=1)


def near_kernel(shards, place_ref, gain_ref, *refs):
    columns, weights = refs[:shards], refs[shards : 3 * shards - 2]
    partial_out, last_out, square_out, project_out, buf = refs[3 * shards - 2 :]
    mine, odd, plane = place_ref[0], place_ref[1], place_ref[2]
    square = 0.0
    for m in range(shards):
        rows = columns[m][...].astype(jnp.float32)
        square += jnp.sum(rows * rows, axis=-1, keepdims=True)
        gain = gain_ref[2 * (plane ^ m) + odd].astype(jnp.float32)
        buf[m] = (rows * gain).astype(jnp.bfloat16)
    square_out[...] = jnp.broadcast_to(square, square_out.shape)
    partial_out[...] = sum(
        product(buf[mine ^ j], weights[2 * j], weights[2 * j + 1]) for j in range(shards - 1)
    )
    last_out[...] = buf[mine ^ (shards - 1)]
    depth = project_out.shape[1]
    high = upper(depth)
    for j in range(shards - 1):
        project_out[j, :high] = weights[2 * j][weights[2 * j].shape[0] - high :]
        project_out[j, high:] = weights[2 * j + 1][weights[2 * j + 1].shape[0] - depth + high :]


def near_products(place, gain, columns, weights, depth):
    shards = len(columns)
    rows, width = columns[0].shape
    return call(
        functools.partial(near_kernel, shards),
        (
            like((rows, 3 * width), jnp.float32),
            like((rows, width)),
            like((rows, 128), jnp.float32),
            like((shards - 1, depth, weights[0].shape[1])),
        ),
        [SM, VM] + [VM] * (3 * shards - 2),
        scratch=[pltpu.VMEM((shards, rows, width), jnp.bfloat16)],
        busy=0.1,
        name="near_products",
    )(place, gain.reshape(2 * shards, 1, width), *columns, *weights)


def far_kernel(partial_ref, last_ref, square_ref, top_ref, bottom_ref, keep_out, send_out):
    total = partial_ref[...] + product(last_ref[...], top_ref, bottom_ref)
    tokens = keep_out.shape[0]
    width = total.shape[1]
    for out, first in ((keep_out, 0), (send_out, tokens)):
        out[:, :width] = total[first : first + tokens]
        out[:, width:] = square_ref[first : first + tokens, :]


def far_products(partial, last, square, top, bottom):
    rows, width = partial.shape
    out = like((rows // 2, width + 128), jnp.float32)
    return call(
        far_kernel,
        (out, out),
        [VM] * 5,
        busy=0.1,
        name="far_products",
    )(partial, last, square, top, bottom)


def rotate(rows, cosine, sine):
    lane = lax.broadcasted_iota(jnp.int32, (rows.shape[0], 128), 1)
    front = (lane % HD) < HD // 2
    slabs = []
    for s in range(rows.shape[1] // 128):
        slab = rows[:, s * 128 : (s + 1) * 128]
        other = jnp.where(
            front, -pltpu.roll(slab, 128 - HD // 2, 1), pltpu.roll(slab, HD // 2, 1)
        )
        slabs.append(slab * cosine + other * sine)
    return slabs


def place_queries(slabs, q_ref):
    rows = slabs[0].shape[0]
    factor = HD ** (-0.5) * math.log2(math.e)
    low = lax.broadcasted_iota(jnp.int32, (rows, 128), 1) < HD
    head = 0
    for s, slab in enumerate(slabs):
        slab = slab * factor
        rolled = pltpu.roll(slab, HD, 1)
        for odd_head in (0, 1):
            group = 0 if s < len(slabs) // 2 else 1
            keep = low if group == 0 else jnp.logical_not(low)
            value = jnp.where(keep, slab if group == odd_head else rolled, 0.0)
            q_ref[head * rows : (head + 1) * rows, :] = value.astype(jnp.bfloat16)
            head += 1


def one_over(x):
    near = pl.reciprocal(x, approx=True)
    return near * (2.0 - x * near)


def attend(q_ref, keys, values, mask):
    tokens = mask.shape[0]
    low = lax.broadcasted_iota(jnp.int32, values.shape, 1) < HD
    one = jnp.ones_like(values)
    mine = [jnp.where(low, values, one), jnp.where(low, one, values)]
    queries = q_ref.shape[0]
    mask = jnp.tile(mask, (QUERY_ROWS // tokens, 1))

    def score(start):
        return lax.dot_general(
            q_ref[start : start + QUERY_ROWS, :],
            keys,
            (((1,), (1,)), ((), ())),
            preferred_element_type=jnp.float32,
        )

    heads = []
    upcoming = score(0)
    for start in range(0, queries, QUERY_ROWS):
        scores = upcoming
        if start + QUERY_ROWS < queries:
            upcoming = score(start + QUERY_ROWS)
        sure = scores.shape[1] - mask.shape[1]
        unsure = jnp.where(mask, scores[:, sure:], masked_score)
        scores = jnp.concatenate([scores[:, :sure], unsure], axis=1) if sure else unsure
        peak = jnp.max(scores, axis=-1, keepdims=True)
        weights = jnp.exp2(scores - peak).astype(jnp.bfloat16)
        total = jnp.dot(
            weights, mine[start * 2 // queries], preferred_element_type=jnp.float32
        )
        mixed = total * one_over(pltpu.roll(total, HD, 1))
        heads += [mixed[i : i + tokens] for i in range(0, QUERY_ROWS, tokens)]
    return heads


def lay_out(heads, out_ref):
    low = lax.broadcasted_iota(jnp.int32, heads[0].shape, 1) < HD
    slabs = []
    for h, mixed in enumerate(heads):
        straight = (h % 2 == 0) == (h < len(heads) // 2)
        slabs.append(mixed if straight else pltpu.roll(mixed, HD, 1))
    for s in range(len(heads) // 2):
        both = jnp.where(low, slabs[2 * s], slabs[2 * s + 1])
        out_ref[:, s * 128 : (s + 1) * 128] = both.astype(jnp.bfloat16)


def attention_kernel(
    features,
    kv_width,
    length_ref,
    cos_ref,
    sin_ref,
    here_ref,
    there_ref,
    k_ref,
    v_ref,
    out_ref,
    nk_out,
    nv_out,
    nk_ref,
    nv_ref,
    q_ref,
    out_sems,
):
    length = length_ref[0]
    total = here_ref[...] + there_ref[...]
    width = total.shape[1] - 128
    scale = lax.rsqrt(total[:, width:] / features + norm_eps)
    total = total[:, :width] * jnp.tile(scale, (1, width // 128))
    tokens = total.shape[0]
    q_width = width - 2 * kv_width
    cosine, sine = cos_ref[...], sin_ref[...]
    (keys,) = rotate(total[:, q_width : q_width + kv_width], cosine, sine)
    nk_ref[...] = keys.astype(jnp.bfloat16)
    nv_ref[...] = total[:, q_width + kv_width :].astype(jnp.bfloat16)
    fresh = fetch([(nk_ref, nk_out), (nv_ref, nv_out)], out_sems)
    place_queries(rotate(total[:, :q_width], cosine, sine), q_ref)

    step = k_ref.shape[0] // CACHE_STEPS
    for cached in range(step, k_ref.shape[0] + 1, step):

        @pl.when((length > cached - step) & (length <= cached))
        def _(cached=cached):
            shape = (tokens, step + tokens)
            column = cached - step + lax.broadcasted_iota(jnp.int32, shape, 1)
            token = lax.broadcasted_iota(jnp.int32, shape, 0)
            limit = jnp.where(column < cached, length, cached + 1 + token)
            heads = attend(
                q_ref,
                jnp.concatenate([k_ref[:cached, :], nk_ref[...]], axis=0),
                jnp.concatenate([v_ref[:cached, :], nv_ref[...]], axis=0),
                column < limit,
            )
            lay_out(heads, out_ref)

    for copy in fresh:
        copy.wait()


def attention(length, features, cosine, sine, here, there, keys, values):
    tokens = here.shape[0]
    kv_width = keys.shape[1]
    q_width = here.shape[1] - 128 - 2 * kv_width
    queries = q_width // HD * tokens
    fresh = like((tokens, kv_width))
    return call(
        functools.partial(attention_kernel, features, kv_width),
        (like((tokens, q_width)), fresh, fresh),
        [SM, VM, VM, VM, VM, VM, VM],
        out_specs=(VM, HB, HB),
        scratch=[
            pltpu.VMEM(fresh.shape, jnp.bfloat16),
            pltpu.VMEM(fresh.shape, jnp.bfloat16),
            pltpu.VMEM((queries, 128), jnp.bfloat16),
            pltpu.SemaphoreType.DMA((2,)),
        ],
        busy=4.0,
        name="attention",
    )(length, cosine, sine, here, there, keys, values)


def out_kernel(distances, chips, place_ref, mixed_ref, own_ref, sibling_ref, *refs):
    last, outs = refs[:4], refs[4:]
    mine, odd = place_ref[0], place_ref[1]
    mixed = mixed_ref[...]
    width = outs[0].shape[1] // 2

    def store(out, weights):
        terms = [
            jnp.dot(mixed, w, preferred_element_type=jnp.float32).astype(jnp.bfloat16)
            for w in weights
        ]
        out[:, :width] = jnp.where(odd == 0, terms[0], terms[1])
        out[:, width:] = jnp.where(odd == 0, terms[1], terms[0])

    for out, m in zip(outs, distances, strict=True):
        j = mine ^ m

        @pl.when(j < chips - 1)
        def _(out=out, j=j):
            store(out, [own_ref[j], sibling_ref[j]])

        @pl.when(j == chips - 1)
        def _(out=out):
            halves = [h[h.shape[0] - last[2 + i % 2].shape[0] :] for i, h in enumerate(last)]
            store(out, [jnp.concatenate(halves[:2], axis=0), jnp.concatenate(halves[2:], axis=0)])


def project(distances, mixed, place, own, sibling, last):
    rows = mixed.shape[0]
    width = own.shape[2]
    return call(
        functools.partial(out_kernel, distances, own.shape[0] + 1),
        tuple(like((rows, 2 * width)) for _ in distances),
        [SM] + [VM] * 7,
        busy=1.0,
        name="project",
    )(place, mixed, own, sibling, *last)


def phases(length_now, row_count):
    positions = (length_now + jnp.arange(row_count, dtype=jnp.int32)).astype(jnp.float32)
    inverse = rope_base ** (-jnp.arange(0, HD, 2, dtype=jnp.int32).astype(jnp.float32) / HD)
    phase = positions[:, None] * jnp.tile(inverse, 4)[None, :]
    return jnp.cos(phase), jnp.sin(phase)


def swap(x, axis, mask):
    count = lax.axis_size(axis)
    return lax.ppermute(x, axis, [(i, i ^ mask) for i in range(count)])


CORE, SIDE_X, SIDE_Y = 1, 2, 4


def core(x):
    return swap(x, "req", CORE)


def per_device(
    hidden, norm_gain, w_query, w_key, w_value, w_out, cache_keys, cache_values, cache_lengths
):
    chip = lax.axis_index("req") // 2
    odd = lax.axis_index("req") % 2
    plane = lax.axis_index("tp")
    place = jnp.stack([chip ^ plane, odd, plane])
    length = lax.dynamic_slice_in_dim(cache_lengths, lax.axis_index("req"), 1, 0)
    tokens = hidden.shape[1]

    top, bottom, keep, send = pack(hidden[0], w_query, w_key, w_value, w_out)
    x_top, y_bottom = swap(top, "req", SIDE_X), swap(bottom, "req", SIDE_Y)
    got, top_later, bottom_later = lax.optimization_barrier((core(send), top, bottom))
    x_bottom, y_top = swap(bottom_later, "req", SIDE_X), swap(top_later, "req", SIDE_Y)
    columns = jnp.concatenate([keep, got], axis=0)
    two = swap(columns, "tp", 2)
    d_top, d_bottom = swap(x_top, "req", SIDE_Y), swap(y_bottom, "req", SIDE_X)
    _, _, columns_later, two_later = lax.optimization_barrier((x_top, y_bottom, columns, two))
    one = swap(columns_later, "tp", 1)
    _, two_later = lax.optimization_barrier((x_bottom, two_later))
    three = swap(two_later, "tp", 1)

    partial, last, square, o_near = near_products(
        place,
        norm_gain,
        [columns, one, two, three],
        [top, bottom, x_top, x_bottom, y_top, y_bottom],
        w_out.shape[0],
    )
    cosine, sine = phases(length[0], tokens)
    partial, cosine, sine = lax.optimization_barrier((partial, cosine, sine))
    here, there = far_products(partial, last, square, d_top, d_bottom)
    there, o_near = lax.optimization_barrier((there, o_near))
    mixed, new_keys, new_values = attention(
        length,
        norm_gain.shape[0],
        cosine,
        sine,
        here,
        core(there),
        cache_keys[0],
        cache_values[0],
    )
    o_sibling = core(o_near)
    high = upper(w_out.shape[0])
    first, second = d_top.shape[0] - high, d_bottom.shape[0] - w_out.shape[0] + high
    o_last = [d_top, d_bottom, core(d_top[first:]), core(d_bottom[second:])]
    terms = {}
    terms[2], terms[3] = project((2, 3,), mixed, place, o_near, o_sibling, o_last)
    mixed, terms[2], terms[3] = lax.optimization_barrier((mixed, terms[2], terms[3]))
    terms[0], terms[1] = project((0, 1,), mixed, place, o_near, o_sibling, o_last)
    total = terms[0].astype(jnp.float32)
    for m in (3, 1, 2):
        total = total + swap(terms[m], "tp", m).astype(jnp.float32)
    return total.astype(jnp.bfloat16)[None], new_keys[None], new_values[None]


def general_rotate(tensor, cosine_table, sine_table):
    half_width = tensor.shape[-1] // 2
    front_half = tensor[..., :half_width]
    back_half = tensor[..., half_width:]
    return jnp.concatenate(
        [
            front_half * cosine_table - back_half * sine_table,
            back_half * cosine_table + front_half * sine_table,
        ],
        axis=-1,
    )


def general_phases(length_now, row_count):
    cosine, sine = phases(length_now, row_count)
    return cosine[:, None, : HD // 2], sine[:, None, : HD // 2]


def group_queries(flat_queries, key_heads, group_size, head_width):
    token_count = flat_queries.shape[0]
    shaped = flat_queries.reshape(token_count, key_heads, group_size, head_width).transpose(
        1, 2, 0, 3
    )
    return shaped.reshape(key_heads, group_size * token_count, head_width)


def attend_block(running, grouped, key_block, value_block, visible):
    peak_old, total_old, accum_old = running
    scores = jnp.einsum(
        "gqd,kgd->gqk", grouped, key_block, preferred_element_type=jnp.float32
    ) * grouped.shape[-1] ** (-0.5)
    scores = jnp.where(visible, scores, masked_score)
    peak_new = jnp.maximum(peak_old, jnp.max(scores, axis=-1))
    weights = jnp.where(visible, jnp.exp(scores - peak_new[..., None]), 0.0)
    factor = jnp.exp(peak_old - peak_new)
    total_new = total_old * factor + jnp.sum(weights, axis=-1)
    accum_new = accum_old * factor[:, None, :] + jnp.einsum(
        "gqk,kgd->gdq",
        weights.astype(jnp.bfloat16),
        value_block,
        preferred_element_type=jnp.float32,
    )
    return (peak_new, total_new, accum_new)


def cache_pass(
    running, grouped, key_cache, value_cache, buffer_first, lower_row, upper_row, block_rows
):
    first_block = lower_row // block_rows
    last_block = jnp.where(
        lower_row < upper_row, (upper_row + block_rows - 1) // block_rows, first_block
    )

    def step_body(block_index, running_now):
        position_first = block_index * block_rows
        local_first = position_first - buffer_first
        key_block = lax.dynamic_slice_in_dim(key_cache, local_first, block_rows, 0)
        value_block = lax.dynamic_slice_in_dim(value_cache, local_first, block_rows, 0)
        positions = position_first + jnp.arange(block_rows, dtype=jnp.int32)
        visible = ((positions >= lower_row) & (positions < upper_row))[None, None, :]
        return attend_block(running_now, grouped, key_block, value_block, visible)

    return lax.fori_loop(first_block, last_block, step_body, running)


def new_pass(running, grouped, fresh_keys, fresh_values, token_count, block_rows):
    token_of_row = jnp.arange(grouped.shape[1], dtype=jnp.int32) % token_count
    positions = 0 + jnp.arange(block_rows, dtype=jnp.int32)
    visible = (positions[None, :] <= token_of_row[:, None])[None]
    running = attend_block(running, grouped, fresh_keys, fresh_values, visible)
    return running


def general_device(
    hidden, norm_gain, w_query, w_key, w_value, w_out, cache_keys, cache_values, cache_lengths
):
    token_count = hidden.shape[1]
    gathered = lax.all_gather(hidden[0], "tp", axis=1, tiled=True)
    as_float = gathered.astype(jnp.float32)
    mean_square = jnp.mean(as_float * as_float, axis=-1, keepdims=True)
    normed = (as_float * lax.rsqrt(mean_square + norm_eps) * norm_gain.astype(jnp.float32)).astype(
        jnp.bfloat16
    )
    query_width = w_query.shape[1]
    key_width = w_key.shape[1]
    query_sum = jnp.dot(
        normed,
        lax.all_gather(w_query, "req", axis=0, tiled=True),
        preferred_element_type=jnp.float32,
    )
    key_sum = jnp.dot(
        normed, lax.all_gather(w_key, "req", axis=0, tiled=True), preferred_element_type=jnp.float32
    )
    value_sum = jnp.dot(
        normed,
        lax.all_gather(w_value, "req", axis=0, tiled=True),
        preferred_element_type=jnp.float32,
    )
    device_index = lax.axis_index("req")
    length_own = cache_lengths[device_index]
    head_width = HD
    local_heads = query_width // head_width
    key_heads = key_width // head_width
    group_size = local_heads // key_heads
    cosine_table, sine_table = general_phases(length_own, token_count)
    flat_queries = (
        general_rotate(query_sum.reshape(token_count, local_heads, head_width), cosine_table, sine_table)
        .astype(jnp.bfloat16)
        .reshape(token_count, query_width)
    )
    fresh_keys = general_rotate(
        key_sum.reshape(token_count, key_heads, head_width), cosine_table, sine_table
    ).astype(jnp.bfloat16)
    fresh_values = value_sum.reshape(token_count, key_heads, head_width).astype(jnp.bfloat16)
    grouped = group_queries(flat_queries, key_heads, group_size, head_width)
    cache_rows = cache_keys.shape[1]
    key_cache = cache_keys[0].reshape(cache_rows, key_heads, head_width)
    value_cache = cache_values[0].reshape(cache_rows, key_heads, head_width)
    block_cache = min(512, cache_rows // 2)
    block_new = min(512, token_count)
    query_count = group_size * token_count
    start_state = (
        jnp.full((key_heads, query_count), masked_score, jnp.float32),
        jnp.zeros((key_heads, query_count), jnp.float32),
        jnp.zeros((key_heads, head_width, query_count), jnp.float32),
    )
    own_part = cache_pass(
        start_state, grouped, key_cache, value_cache, 0, 0, length_own, block_cache
    )
    combined = new_pass(own_part, grouped, fresh_keys, fresh_values, token_count, block_new)
    accumulated = combined[2] / combined[1][:, None, :]
    mixed_heads = (
        accumulated.reshape(key_heads, head_width, group_size, token_count)
        .transpose(3, 0, 2, 1)
        .reshape(token_count, query_width)
        .astype(jnp.bfloat16)
    )
    partial_out = jnp.dot(
        mixed_heads,
        lax.all_gather(w_out, "req", axis=1, tiled=True),
        preferred_element_type=jnp.float32,
    )
    summed = lax.psum_scatter(
        partial_out.astype(jnp.bfloat16), "tp", scatter_dimension=1, tiled=True
    )
    return (
        summed[None],
        fresh_keys.reshape(token_count, key_width)[None],
        fresh_values.reshape(token_count, key_width)[None],
    )


def solution(mesh):
    in_specs = (
        P("req", None, "tp"),
        P(),
        P("req", "tp"),
        P("req", "tp"),
        P("req", "tp"),
        P("tp", "req"),
        P("req", None, "tp"),
        P("req", None, "tp"),
        P(),
    )
    out_specs = (P("req", None, "tp"), P("req", None, "tp"), P("req", None, "tp"))
    ringed = mesh.shape["req"] == 8 and mesh.shape["tp"] == 4
    return jax.shard_map(
        per_device if ringed else general_device,
        mesh=mesh,
        in_specs=in_specs,
        out_specs=out_specs,
        check_vma=False,
    )
```

```python
import functools
import math

import jax
import jax.numpy as jnp
from jax import lax
from jax.experimental import pallas as pl
from jax.experimental.pallas import tpu as pltpu
from jax.sharding import PartitionSpec as P

HD = 64
rope_base = 1000000.0
norm_eps = 1e-05
masked_score = -1e30
CACHE_STEPS = 8
QUERY_ROWS = 512
SIXTEENTHS = 8
FLOPS_PER_US = 1.1e9
VMEM_BYTES = 24 * 1024 * 1024

VM = pl.BlockSpec(memory_space=pltpu.VMEM)
HB = pl.BlockSpec(memory_space=pltpu.HBM)
SM = pl.BlockSpec(memory_space=pltpu.SMEM)


def call(kernel, out_shape, in_specs, scratch=(), busy=1.0, name=None, out_specs=None):
    run = pl.pallas_call(
        kernel,
        out_shape=out_shape,
        in_specs=in_specs,
        out_specs=out_specs or jax.tree.map(lambda _: VM, out_shape),
        scratch_shapes=list(scratch),
        compiler_params=pltpu.CompilerParams(vmem_limit_bytes=VMEM_BYTES),
        cost_estimate=pl.CostEstimate(
            flops=int(busy * FLOPS_PER_US), bytes_accessed=1 << 16, transcendentals=0
        ),
        name=name,
    )

    def placed(*operands):
        return run(
            *[
                pltpu.with_memory_space_constraint(x, pltpu.HBM) if spec is HB else x
                for x, spec in zip(operands, in_specs, strict=True)
            ]
        )

    return placed


def like(shape, dtype=jnp.bfloat16):
    return jax.ShapeDtypeStruct(shape, dtype)


def fetch(pairs, sems):
    copies = [pltpu.make_async_copy(src, dst, sems.at[i]) for i, (src, dst) in enumerate(pairs)]
    for copy in copies:
        copy.start()
    return copies


def upper(rows):
    return rows * SIXTEENTHS // 16


def pack_kernel(
    hidden_ref,
    wq_ref,
    wk_ref,
    wv_ref,
    wo_ref,
    top_out,
    bottom_out,
    keep_out,
    send_out,
    sems,
):
    odd = lax.axis_index("req") % 2
    rows, width = wq_ref.shape
    column, kv = top_out.shape[1], wk_ref.shape[1]
    pairs = []
    for part, out in enumerate((top_out, bottom_out)):
        start, size = part * upper(rows), (upper(rows), rows - upper(rows))[part]
        source = pl.ds(start, size)
        first = 0
        for c in range(width // column):
            pairs.append((wq_ref.at[source, pl.ds(c * column, column)], out.at[pl.ds(first, size)]))
            first += size
        for i, w in enumerate((wk_ref, wv_ref)):
            pairs.append((w.at[source], out.at[pl.ds(first, size), pl.ds(i * kv, kv)]))
        first += size
        depth = wo_ref.shape[0]
        start, size = part * upper(depth), (upper(depth), depth - upper(depth))[part]
        pairs.append((wo_ref.at[pl.ds(start, size)], out.at[pl.ds(first, size)]))
    half = keep_out.shape[1]
    mine = pl.ds(pl.multiple_of(odd * half, half), half)
    other = pl.ds(pl.multiple_of((1 - odd) * half, half), half)
    pairs += [(hidden_ref.at[:, other], send_out), (hidden_ref.at[:, mine], keep_out)]
    for copy in fetch(pairs, sems):
        copy.wait()


def pack(hidden, w_query, w_key, w_value, w_out):
    column = 2 * w_key.shape[1]
    blocks = w_query.shape[1] // column + 1
    rows = w_query.shape[0] * blocks + w_out.shape[0]
    top = upper(w_query.shape[0]) * blocks + upper(w_out.shape[0])
    columns = like((hidden.shape[0], hidden.shape[1] // 2))
    return call(
        pack_kernel,
        (like((top, column)), like((rows - top, column)), columns, columns),
        [HB] * 5,
        scratch=[pltpu.SemaphoreType.DMA((12,))],
        name="pack",
    )(hidden, w_query, w_key, w_value, w_out)


def product(rows, top_ref, bottom_ref):
    depth = rows.shape[1]
    high, low = upper(depth), depth - upper(depth)
    parts = []
    for c in range(3):
        block = jnp.concatenate(
            [top_ref[c * high : (c + 1) * high], bottom_ref[c * low : (c + 1) * low]], axis=0
        )
        parts.append(jnp.dot(rows, block, preferred_element_type=jnp.float32))
    return jnp.concatenate(parts, axis=1)


def near_kernel(shards, place_ref, gain_ref, *refs):
    columns, weights = refs[:shards], refs[shards : 3 * shards - 2]
    partial_out, last_out, square_out, project_out, buf = refs[3 * shards - 2 :]
    mine, odd, plane = place_ref[0], place_ref[1], place_ref[2]
    square = 0.0
    for m in range(shards):
        rows = columns[m][...].astype(jnp.float32)
        square += jnp.sum(rows * rows, axis=-1, keepdims=True)
        gain = gain_ref[2 * (plane ^ m) + odd].astype(jnp.float32)
        buf[m] = (rows * gain).astype(jnp.bfloat16)
    square_out[...] = jnp.broadcast_to(square, square_out.shape)
    partial_out[...] = sum(
        product(buf[mine ^ j], weights[2 * j], weights[2 * j + 1]) for j in range(shards - 1)
    )
    last_out[...] = buf[mine ^ (shards - 1)]
    depth = project_out.shape[1]
    high = upper(depth)
    for j in range(shards - 1):
        project_out[j, :high] = weights[2 * j][weights[2 * j].shape[0] - high :]
        project_out[j, high:] = weights[2 * j + 1][weights[2 * j + 1].shape[0] - depth + high :]


def near_products(place, gain, columns, weights, depth):
    shards = len(columns)
    rows, width = columns[0].shape
    return call(
        functools.partial(near_kernel, shards),
        (
            like((rows, 3 * width), jnp.float32),
            like((rows, width)),
            like((rows, 128), jnp.float32),
            like((shards - 1, depth, weights[0].shape[1])),
        ),
        [SM, VM] + [VM] * (3 * shards - 2),
        scratch=[pltpu.VMEM((shards, rows, width), jnp.bfloat16)],
        busy=0.1,
        name="near_products",
    )(place, gain.reshape(2 * shards, 1, width), *columns, *weights)


def far_kernel(partial_ref, last_ref, top_ref, bottom_ref, keep_out, send_out):
    total = partial_ref[...] + product(last_ref[...], top_ref, bottom_ref)
    tokens = keep_out.shape[0]
    for out, first in ((keep_out, 0), (send_out, tokens)):
        out[...] = total[first : first + tokens]


def far_products(partial, last, top, bottom):
    rows, width = partial.shape
    out = like((rows // 2, width), jnp.float32)
    return call(
        far_kernel,
        (out, out),
        [VM] * 4,
        busy=0.1,
        name="far_products",
    )(partial, last, top, bottom)


def rotate(rows, cosine, sine):
    lane = lax.broadcasted_iota(jnp.int32, (rows.shape[0], 128), 1)
    front = (lane % HD) < HD // 2
    slabs = []
    for s in range(rows.shape[1] // 128):
        slab = rows[:, s * 128 : (s + 1) * 128]
        other = jnp.where(
            front, -pltpu.roll(slab, 128 - HD // 2, 1), pltpu.roll(slab, HD // 2, 1)
        )
        slabs.append(slab * cosine + other * sine)
    return slabs


def place_queries(slabs, q_ref):
    rows = slabs[0].shape[0]
    factor = HD ** (-0.5) * math.log2(math.e)
    low = lax.broadcasted_iota(jnp.int32, (rows, 128), 1) < HD
    head = 0
    for s, slab in enumerate(slabs):
        slab = slab * factor
        rolled = pltpu.roll(slab, HD, 1)
        for odd_head in (0, 1):
            group = 0 if s < len(slabs) // 2 else 1
            keep = low if group == 0 else jnp.logical_not(low)
            value = jnp.where(keep, slab if group == odd_head else rolled, 0.0)
            q_ref[head * rows : (head + 1) * rows, :] = value.astype(jnp.bfloat16)
            head += 1


def one_over(x):
    near = pl.reciprocal(x, approx=True)
    return near * (2.0 - x * near)


def attend(q_ref, keys, values, mask):
    tokens = mask.shape[0]
    low = lax.broadcasted_iota(jnp.int32, values.shape, 1) < HD
    one = jnp.ones_like(values)
    mine = [jnp.where(low, values, one), jnp.where(low, one, values)]
    queries = q_ref.shape[0]
    mask = jnp.tile(mask, (QUERY_ROWS // tokens, 1))

    def score(start):
        return lax.dot_general(
            q_ref[start : start + QUERY_ROWS, :],
            keys,
            (((1,), (1,)), ((), ())),
            preferred_element_type=jnp.float32,
        )

    heads = []
    upcoming = score(0)
    for start in range(0, queries, QUERY_ROWS):
        scores = upcoming
        if start + QUERY_ROWS < queries:
            upcoming = score(start + QUERY_ROWS)
        sure = scores.shape[1] - mask.shape[1]
        unsure = jnp.where(mask, scores[:, sure:], masked_score)
        scores = jnp.concatenate([scores[:, :sure], unsure], axis=1) if sure else unsure
        peak = jnp.max(scores, axis=-1, keepdims=True)
        weights = jnp.exp2(scores - peak).astype(jnp.bfloat16)
        total = jnp.dot(
            weights, mine[start * 2 // queries], preferred_element_type=jnp.float32
        )
        mixed = total * one_over(pltpu.roll(total, HD, 1))
        heads += [mixed[i : i + tokens] for i in range(0, QUERY_ROWS, tokens)]
    return heads


def lay_out(heads, out_ref):
    low = lax.broadcasted_iota(jnp.int32, heads[0].shape, 1) < HD
    slabs = []
    for h, mixed in enumerate(heads):
        straight = (h % 2 == 0) == (h < len(heads) // 2)
        slabs.append(mixed if straight else pltpu.roll(mixed, HD, 1))
    for s in range(len(heads) // 2):
        both = jnp.where(low, slabs[2 * s], slabs[2 * s + 1])
        out_ref[:, s * 128 : (s + 1) * 128] = both.astype(jnp.bfloat16)


def attention_kernel(
    features,
    kv_width,
    length_ref,
    cos_ref,
    sin_ref,
    here_ref,
    there_ref,
    square_here_ref,
    square_there_ref,
    k_ref,
    v_ref,
    out_ref,
    nk_out,
    nv_out,
    nk_ref,
    nv_ref,
    q_ref,
    out_sems,
):
    length = length_ref[0]
    total = here_ref[...] + there_ref[...]
    width = total.shape[1]
    square = square_here_ref[: total.shape[0]] + square_there_ref[...]
    scale = lax.rsqrt(square / features + norm_eps)
    total = total * jnp.tile(scale, (1, width // 128))
    tokens = total.shape[0]
    q_width = width - 2 * kv_width
    cosine, sine = cos_ref[...], sin_ref[...]
    (keys,) = rotate(total[:, q_width : q_width + kv_width], cosine, sine)
    nk_ref[...] = keys.astype(jnp.bfloat16)
    nv_ref[...] = total[:, q_width + kv_width :].astype(jnp.bfloat16)
    fresh = fetch([(nk_ref, nk_out), (nv_ref, nv_out)], out_sems)
    place_queries(rotate(total[:, :q_width], cosine, sine), q_ref)

    step = k_ref.shape[0] // CACHE_STEPS
    for cached in range(step, k_ref.shape[0] + 1, step):

        @pl.when((length > cached - step) & (length <= cached))
        def _(cached=cached):
            shape = (tokens, step + tokens)
            column = cached - step + lax.broadcasted_iota(jnp.int32, shape, 1)
            token = lax.broadcasted_iota(jnp.int32, shape, 0)
            limit = jnp.where(column < cached, length, cached + 1 + token)
            heads = attend(
                q_ref,
                jnp.concatenate([k_ref[:cached, :], nk_ref[...]], axis=0),
                jnp.concatenate([v_ref[:cached, :], nv_ref[...]], axis=0),
                column < limit,
            )
            lay_out(heads, out_ref)

    for copy in fresh:
        copy.wait()


def attention(length, features, cosine, sine, here, there, square, square_there, keys, values):
    tokens = here.shape[0]
    kv_width = keys.shape[1]
    q_width = here.shape[1] - 2 * kv_width
    queries = q_width // HD * tokens
    fresh = like((tokens, kv_width))
    return call(
        functools.partial(attention_kernel, features, kv_width),
        (like((tokens, q_width)), fresh, fresh),
        [SM] + [VM] * 8,
        out_specs=(VM, HB, HB),
        scratch=[
            pltpu.VMEM(fresh.shape, jnp.bfloat16),
            pltpu.VMEM(fresh.shape, jnp.bfloat16),
            pltpu.VMEM((queries, 128), jnp.bfloat16),
            pltpu.SemaphoreType.DMA((2,)),
        ],
        busy=4.0,
        name="attention",
    )(length, cosine, sine, here, there, square, square_there, keys, values)


def out_kernel(distances, chips, place_ref, mixed_ref, own_ref, sibling_ref, *refs):
    last, outs = refs[:4], refs[4:]
    mine, odd = place_ref[0], place_ref[1]
    mixed = mixed_ref[...]
    width = outs[0].shape[1] // 2

    def store(out, weights):
        terms = [
            jnp.dot(mixed, w, preferred_element_type=jnp.float32).astype(jnp.bfloat16)
            for w in weights
        ]
        out[:, :width] = jnp.where(odd == 0, terms[0], terms[1])
        out[:, width:] = jnp.where(odd == 0, terms[1], terms[0])

    for out, m in zip(outs, distances, strict=True):
        j = mine ^ m

        @pl.when(j < chips - 1)
        def _(out=out, j=j):
            store(out, [own_ref[j], sibling_ref[j]])

        @pl.when(j == chips - 1)
        def _(out=out):
            halves = [h[h.shape[0] - last[2 + i % 2].shape[0] :] for i, h in enumerate(last)]
            store(out, [jnp.concatenate(halves[:2], axis=0), jnp.concatenate(halves[2:], axis=0)])


def project(distances, mixed, place, own, sibling, last):
    rows = mixed.shape[0]
    width = own.shape[2]
    return call(
        functools.partial(out_kernel, distances, own.shape[0] + 1),
        tuple(like((rows, 2 * width)) for _ in distances),
        [SM] + [VM] * 7,
        busy=1.0,
        name="project",
    )(place, mixed, own, sibling, *last)


def phases(length_now, row_count):
    positions = (length_now + jnp.arange(row_count, dtype=jnp.int32)).astype(jnp.float32)
    inverse = rope_base ** (-jnp.arange(0, HD, 2, dtype=jnp.int32).astype(jnp.float32) / HD)
    phase = positions[:, None] * jnp.tile(inverse, 4)[None, :]
    return jnp.cos(phase), jnp.sin(phase)


def swap(x, axis, mask):
    count = lax.axis_size(axis)
    return lax.ppermute(x, axis, [(i, i ^ mask) for i in range(count)])


CORE, SIDE_X, SIDE_Y = 1, 2, 4


def core(x):
    return swap(x, "req", CORE)


def per_device(
    hidden, norm_gain, w_query, w_key, w_value, w_out, cache_keys, cache_values, cache_lengths
):
    chip = lax.axis_index("req") // 2
    odd = lax.axis_index("req") % 2
    plane = lax.axis_index("tp")
    place = jnp.stack([chip ^ plane, odd, plane])
    length = lax.dynamic_slice_in_dim(cache_lengths, lax.axis_index("req"), 1, 0)
    tokens = hidden.shape[1]

    top, bottom, keep, send = pack(hidden[0], w_query, w_key, w_value, w_out)
    x_top, y_bottom = swap(top, "req", SIDE_X), swap(bottom, "req", SIDE_Y)
    got, top_later, bottom_later = lax.optimization_barrier((core(send), top, bottom))
    x_bottom, y_top = swap(bottom_later, "req", SIDE_X), swap(top_later, "req", SIDE_Y)
    columns = jnp.concatenate([keep, got], axis=0)
    two = swap(columns, "tp", 2)
    d_top, d_bottom = swap(x_top, "req", SIDE_Y), swap(y_bottom, "req", SIDE_X)
    _, _, columns_later, two_later = lax.optimization_barrier((x_top, y_bottom, columns, two))
    one = swap(columns_later, "tp", 1)
    _, two_later = lax.optimization_barrier((x_bottom, two_later))
    three = swap(two_later, "tp", 1)

    partial, last, square, o_near = near_products(
        place,
        norm_gain,
        [columns, one, two, three],
        [top, bottom, x_top, x_bottom, y_top, y_bottom],
        w_out.shape[0],
    )
    cosine, sine = phases(length[0], tokens)
    partial, cosine, sine = lax.optimization_barrier((partial, cosine, sine))
    here, there = far_products(partial, last, d_top, d_bottom)
    there, o_near = lax.optimization_barrier((there, o_near))
    mixed, new_keys, new_values = attention(
        length,
        norm_gain.shape[0],
        cosine,
        sine,
        here,
        core(there),
        square,
        core(square[tokens:]),
        cache_keys[0],
        cache_values[0],
    )
    o_sibling = core(o_near)
    high = upper(w_out.shape[0])
    first, second = d_top.shape[0] - high, d_bottom.shape[0] - w_out.shape[0] + high
    o_last = [d_top, d_bottom, core(d_top[first:]), core(d_bottom[second:])]
    terms = {}
    terms[2], terms[3] = project((2, 3,), mixed, place, o_near, o_sibling, o_last)
    mixed, terms[2], terms[3] = lax.optimization_barrier((mixed, terms[2], terms[3]))
    terms[0], terms[1] = project((0, 1,), mixed, place, o_near, o_sibling, o_last)
    total = terms[0].astype(jnp.float32)
    for m in (3, 1, 2):
        total = total + swap(terms[m], "tp", m).astype(jnp.float32)
    return total.astype(jnp.bfloat16)[None], new_keys[None], new_values[None]


def general_rotate(tensor, cosine_table, sine_table):
    half_width = tensor.shape[-1] // 2
    front_half = tensor[..., :half_width]
    back_half = tensor[..., half_width:]
    return jnp.concatenate(
        [
            front_half * cosine_table - back_half * sine_table,
            back_half * cosine_table + front_half * sine_table,
        ],
        axis=-1,
    )


def general_phases(length_now, row_count):
    cosine, sine = phases(length_now, row_count)
    return cosine[:, None, : HD // 2], sine[:, None, : HD // 2]


def group_queries(flat_queries, key_heads, group_size, head_width):
    token_count = flat_queries.shape[0]
    shaped = flat_queries.reshape(token_count, key_heads, group_size, head_width).transpose(
        1, 2, 0, 3
    )
    return shaped.reshape(key_heads, group_size * token_count, head_width)


def attend_block(running, grouped, key_block, value_block, visible):
    peak_old, total_old, accum_old = running
    scores = jnp.einsum(
        "gqd,kgd->gqk", grouped, key_block, preferred_element_type=jnp.float32
    ) * grouped.shape[-1] ** (-0.5)
    scores = jnp.where(visible, scores, masked_score)
    peak_new = jnp.maximum(peak_old, jnp.max(scores, axis=-1))
    weights = jnp.where(visible, jnp.exp(scores - peak_new[..., None]), 0.0)
    factor = jnp.exp(peak_old - peak_new)
    total_new = total_old * factor + jnp.sum(weights, axis=-1)
    accum_new = accum_old * factor[:, None, :] + jnp.einsum(
        "gqk,kgd->gdq",
        weights.astype(jnp.bfloat16),
        value_block,
        preferred_element_type=jnp.float32,
    )
    return (peak_new, total_new, accum_new)


def cache_pass(
    running, grouped, key_cache, value_cache, buffer_first, lower_row, upper_row, block_rows
):
    first_block = lower_row // block_rows
    last_block = jnp.where(
        lower_row < upper_row, (upper_row + block_rows - 1) // block_rows, first_block
    )

    def step_body(block_index, running_now):
        position_first = block_index * block_rows
        local_first = position_first - buffer_first
        key_block = lax.dynamic_slice_in_dim(key_cache, local_first, block_rows, 0)
        value_block = lax.dynamic_slice_in_dim(value_cache, local_first, block_rows, 0)
        positions = position_first + jnp.arange(block_rows, dtype=jnp.int32)
        visible = ((positions >= lower_row) & (positions < upper_row))[None, None, :]
        return attend_block(running_now, grouped, key_block, value_block, visible)

    return lax.fori_loop(first_block, last_block, step_body, running)


def new_pass(running, grouped, fresh_keys, fresh_values, token_count, block_rows):
    token_of_row = jnp.arange(grouped.shape[1], dtype=jnp.int32) % token_count
    positions = 0 + jnp.arange(block_rows, dtype=jnp.int32)
    visible = (positions[None, :] <= token_of_row[:, None])[None]
    running = attend_block(running, grouped, fresh_keys, fresh_values, visible)
    return running


def general_device(
    hidden, norm_gain, w_query, w_key, w_value, w_out, cache_keys, cache_values, cache_lengths
):
    token_count = hidden.shape[1]
    gathered = lax.all_gather(hidden[0], "tp", axis=1, tiled=True)
    as_float = gathered.astype(jnp.float32)
    mean_square = jnp.mean(as_float * as_float, axis=-1, keepdims=True)
    normed = (as_float * lax.rsqrt(mean_square + norm_eps) * norm_gain.astype(jnp.float32)).astype(
        jnp.bfloat16
    )
    query_width = w_query.shape[1]
    key_width = w_key.shape[1]
    query_sum = jnp.dot(
        normed,
        lax.all_gather(w_query, "req", axis=0, tiled=True),
        preferred_element_type=jnp.float32,
    )
    key_sum = jnp.dot(
        normed, lax.all_gather(w_key, "req", axis=0, tiled=True), preferred_element_type=jnp.float32
    )
    value_sum = jnp.dot(
        normed,
        lax.all_gather(w_value, "req", axis=0, tiled=True),
        preferred_element_type=jnp.float32,
    )
    device_index = lax.axis_index("req")
    length_own = cache_lengths[device_index]
    head_width = HD
    local_heads = query_width // head_width
    key_heads = key_width // head_width
    group_size = local_heads // key_heads
    cosine_table, sine_table = general_phases(length_own, token_count)
    flat_queries = (
        general_rotate(query_sum.reshape(token_count, local_heads, head_width), cosine_table, sine_table)
        .astype(jnp.bfloat16)
        .reshape(token_count, query_width)
    )
    fresh_keys = general_rotate(
        key_sum.reshape(token_count, key_heads, head_width), cosine_table, sine_table
    ).astype(jnp.bfloat16)
    fresh_values = value_sum.reshape(token_count, key_heads, head_width).astype(jnp.bfloat16)
    grouped = group_queries(flat_queries, key_heads, group_size, head_width)
    cache_rows = cache_keys.shape[1]
    key_cache = cache_keys[0].reshape(cache_rows, key_heads, head_width)
    value_cache = cache_values[0].reshape(cache_rows, key_heads, head_width)
    block_cache = min(512, cache_rows // 2)
    block_new = min(512, token_count)
    query_count = group_size * token_count
    start_state = (
        jnp.full((key_heads, query_count), masked_score, jnp.float32),
        jnp.zeros((key_heads, query_count), jnp.float32),
        jnp.zeros((key_heads, head_width, query_count), jnp.float32),
    )
    own_part = cache_pass(
        start_state, grouped, key_cache, value_cache, 0, 0, length_own, block_cache
    )
    combined = new_pass(own_part, grouped, fresh_keys, fresh_values, token_count, block_new)
    accumulated = combined[2] / combined[1][:, None, :]
    mixed_heads = (
        accumulated.reshape(key_heads, head_width, group_size, token_count)
        .transpose(3, 0, 2, 1)
        .reshape(token_count, query_width)
        .astype(jnp.bfloat16)
    )
    partial_out = jnp.dot(
        mixed_heads,
        lax.all_gather(w_out, "req", axis=1, tiled=True),
        preferred_element_type=jnp.float32,
    )
    summed = lax.psum_scatter(
        partial_out.astype(jnp.bfloat16), "tp", scatter_dimension=1, tiled=True
    )
    return (
        summed[None],
        fresh_keys.reshape(token_count, key_width)[None],
        fresh_values.reshape(token_count, key_width)[None],
    )


def solution(mesh):
    in_specs = (
        P("req", None, "tp"),
        P(),
        P("req", "tp"),
        P("req", "tp"),
        P("req", "tp"),
        P("tp", "req"),
        P("req", None, "tp"),
        P("req", None, "tp"),
        P(),
    )
    out_specs = (P("req", None, "tp"), P("req", None, "tp"), P("req", None, "tp"))
    ringed = mesh.shape["req"] == 8 and mesh.shape["tp"] == 4
    return jax.shard_map(
        per_device if ringed else general_device,
        mesh=mesh,
        in_specs=in_specs,
        out_specs=out_specs,
        check_vma=False,
    )
```
